32 devices in a mesh: groups: 2 (over y), dp: 4 (over z), block: 2 (over x), cores: 2 (over core).
Axes of the slice: x: 2, y: 2, z: 4, core: 2. Of those that a mesh axis runs over, the one named last changes fastest.
Arguments:
- activations: bfloat16 [16, 128, 5120], P(('groups', 'dp'), None, ('block', 'cores')), parts along dimension 0, may hold values from -6 to 6
- gradients: bfloat16 [16, 128, 27648], P(('groups', 'dp'), None, ('block', 'cores')), parts along dimension 0, may hold values from -0.5 to 0.5
- token_counts: int32 [16], P(('groups', 'dp')), parts along dimension 0, may hold values from 1 to 128, 768 in all
- basis_act: bfloat16 [5120, 1536], P(('block', 'cores')), may hold values from -0.078125 to 0.078125
- basis_store: bfloat16 [4, 27648, 128], P('dp', ('block', 'cores')), may hold values from -0.0390625 to 0.0390625
- owner_slot: int32 [4], replicated, may hold values from 0 to 3, each once
- reader_blocks: int32 [4, 2], P(('block', 'cores')), may hold values from 0 to 2, all different within a row
Outputs:
- eigenvalues: float32 [2048, 512], P(('groups', 'dp'), ('block', 'cores')), parts along dimension 0
The draws below stay inside these ranges and needn't reach their ends.
There are 2 independent parts, one for each index of `groups`. The reference program is written for one: setup_inputs(seed, part) draws one part's arguments, and reference() takes and returns one part's arrays. A program takes and returns all parts, laid end to end along the dimension named above; an argument that names none is the same for every part. Nothing has to cross between parts.
Inputs may be any that keep to these rules, and one draw needn't show every extreme that they name: `owner_slot`: each number of 0 to 3 appears once. `reader_blocks`: the 2 numbers of a row differ; every input-side block appears in some row. `token_counts`: within each part they sum to 768 and some sequence uses all 128 slots.
All inputs are finite; a program needn't handle non-finite values. No bound on the sum of `token_counts` on one device may be relied on, other than what follows from the above.
Results may differ from the reference program's by a relative error of at most 0.0017.
Values may be sent and summed in bfloat16 or wider, within the bound.
No kernel may reach another device: no remote copies, remote signals or barrier semaphores. Data moves between devices by JAX's collectives and lax.ppermute only.
A program may use at most 64 MiB of HBM per device.

```python
import math
import jax
import jax.numpy as jnp
import numpy as np
from jax import lax

D = 5120
FF = 27648
BW = 512
AB = 3
RL = 2
GC = 128
LEN = 128
SEQS = 8
NPIECE = 4
AW = 1536


def steps_of(stream_key, dims, split, low, high):
    def one(dim, blocks):
        steps = jax.random.uniform(jax.random.fold_in(jax.random.fold_in(stream_key, 6), dim), (blocks,), jnp.float32, low / len(split), high / len(split))
        return jnp.repeat(jnp.exp(steps), dims[dim] // blocks).reshape((-1,) + (1,) * (len(dims) - dim - 1))

    gain = one(*split[0])
    for cut in split[1:]:
        gain = gain * one(*cut)
    return gain


def different_ones(rng, rows, count, top, lift):
    ranking = jax.random.permutation(jax.random.fold_in(rng, 1), count)
    boost = ranking
    for power in range(3):
        boost = boost * boost // count
    boost = boost * lift // count
    chance = jax.random.randint(jax.random.fold_in(rng, 2), (rows, count), 0, 4096) + boost
    fixed_rows = jax.random.permutation(jax.random.fold_in(rng, 3), rows)[jnp.arange(count) % rows]
    chance = jnp.where(jnp.arange(rows)[:, None] == fixed_rows[None, :], 1 << 14, chance)
    merit = chance * count + jnp.arange(count)
    return lax.top_k(merit.astype(jnp.int32), top)[1].astype(jnp.int32)


def split_up(count, total, most, skew):
    portions = [(1 << 20) // math.isqrt(rank ** skew) + 1 for rank in range(2, count + 1)]
    rest, holding = total - most - (count - 1), [1] * (count - 1)
    while rest > 0:
        candidates = [i for i in range(count - 1) if holding[i] < most]
        whole, left = sum([portions[i] for i in candidates]), rest
        for i in candidates:
            more = min(most - holding[i], max(1, left * portions[i] // whole), rest)
            holding[i] = holding[i] + more
            rest = rest - more
    return np.array([most] + holding)


def ragged(own_key, number_of, total, reach, lean):
    if number_of == 2:
        one = jax.random.randint(own_key, (), max(1, total - reach), min(reach, total - 1) + 1)
        return jnp.stack([one, total - one])
    lengths = jnp.asarray(split_up(number_of, total, reach, lean), jnp.int32)
    twos = (number_of - 1) // 2
    giver, sink = lengths[1:1 + 2 * twos:2], lengths[2:2 + 2 * twos:2]
    slack = jnp.minimum(giver - 1, reach - sink)
    moved = jax.random.randint(jax.random.fold_in(own_key, 1), (twos,), 0, 1 << 20) % (slack + 1)
    lengths = lengths.at[1:1 + 2 * twos:2].set(giver - moved).at[2:2 + 2 * twos:2].set(sink + moved)
    return lengths[jax.random.permutation(jax.random.fold_in(own_key, 2), number_of)]


def scatter_about(stream_key, shape, spread, most, shards=(), kind=jnp.bfloat16):
    level = steps_of(stream_key, shape, shards, -0.22, 0.18) if shards else 1.0
    array = jax.random.normal(stream_key, shape, jnp.float32) * spread * level
    return jnp.minimum(jnp.maximum(array, -most), most).astype(kind)


def setup_inputs(seed: int = 0, part: int = 0) -> dict:
    key_of = jax.random.split(jax.random.key(seed), 8)
    part_splits = jax.random.split(jax.random.fold_in(key_of[7], part), 8)
    activations = scatter_about(part_splits[0], (SEQS, LEN, D), 1.0, 6.0, ((0, 4), (2, 4)))
    gradients = scatter_about(part_splits[1], (SEQS, LEN, FF), 0.0625, 0.5, ((0, 4), (2, 4)))
    token_counts = ragged(part_splits[2], SEQS, (3 * SEQS * LEN) // 4, LEN, 1).astype(jnp.int32)
    basis_act = scatter_about(key_of[3], (D, AW), D ** -0.5, 0.078125, ((0, 4),))
    basis_store = scatter_about(key_of[4], (NPIECE, FF, GC), FF ** -0.5, 0.0390625, ((0, 4), (1, 4)))
    owner_slot = jax.random.permutation(key_of[5], NPIECE).astype(jnp.int32)
    reader_blocks = different_ones(key_of[6], NPIECE, AB, RL, 0)
    return dict(activations=activations, gradients=gradients, token_counts=token_counts, basis_act=basis_act, basis_store=basis_store, owner_slot=owner_slot, reader_blocks=reader_blocks)


def reference(activations, gradients, token_counts, basis_act, basis_store, owner_slot, reader_blocks):
    positions = jnp.arange(LEN, dtype=jnp.int32)
    in_range = (positions[None, :] < token_counts[:, None]).astype(jnp.bfloat16)
    flat_acts = activations.reshape(SEQS * LEN, D)
    act_rot = jnp.dot(flat_acts, basis_act, preferred_element_type=jnp.float32).astype(jnp.bfloat16)
    masked = (gradients * in_range[:, :, None]).reshape(SEQS * LEN, FF)

    def rotate_piece(slot):
        piece = lax.dynamic_index_in_dim(basis_store, slot, 0, keepdims=False)
        return jnp.dot(masked, piece, preferred_element_type=jnp.float32).astype(jnp.bfloat16)

    grad_rot = lax.map(rotate_piece, owner_slot)

    def piece_values(piece_index):
        blocks = lax.dynamic_index_in_dim(reader_blocks, piece_index, 0, keepdims=False)
        chosen = jnp.concatenate(
            [lax.dynamic_slice_in_dim(act_rot, (blocks[r] * BW).astype(jnp.int32), BW, 1) for r in range(RL)], axis=1)
        chosen = chosen.reshape(SEQS, LEN, RL * BW).astype(jnp.float32)
        rotated = lax.dynamic_index_in_dim(grad_rot, piece_index, 0, keepdims=False)
        rotated = rotated.reshape(SEQS, LEN, GC).astype(jnp.float32)
        products = jnp.einsum('slr,slc->src', chosen, rotated)
        return jnp.sum(products * products, axis=0) / SEQS

    values = lax.map(piece_values, jnp.arange(NPIECE, dtype=jnp.int32))
    return jnp.transpose(values, (1, 0, 2)).reshape(RL * BW, NPIECE * GC)
```

```python
import jax
import jax.numpy as jnp
from jax import lax
from jax.sharding import PartitionSpec as P

BW = 512
LEN = 128
F32 = jnp.float32
BF16 = jnp.bfloat16


def shift(value, axis, step):
    size = lax.axis_size(axis)
    return lax.ppermute(value, axis, [(i, (i + step) % size) for i in range(size)])


def block_of(value, index):
    return lax.dynamic_index_in_dim(value, index, 0, keepdims=False)


def reduce_scatter(blocks, axis, wire=F32):
    size, me = lax.axis_size(axis), lax.axis_index(axis)
    total = block_of(blocks, me)
    for step in range(1, size):
        term = block_of(blocks, (me + step) % size).astype(wire)
        total = total + shift(term, axis, step).astype(F32)
    return total


def gather(block, axis):
    size, me = lax.axis_size(axis), lax.axis_index(axis)
    out = jnp.zeros((size,) + block.shape, block.dtype)
    out = lax.dynamic_update_index_in_dim(out, block, me, 0)
    for step in range(1, size):
        came = shift(block, axis, step)
        out = lax.dynamic_update_index_in_dim(out, came, (me - step) % size, 0)
    return out


def on_device(
    activations, gradients, token_counts, basis_act, basis_store, owner_slot, reader_blocks
):
    seq_local = activations.shape[0]
    slots = seq_local * LEN
    groups, dp = lax.axis_size("groups"), lax.axis_size("dp")
    cores, blocks = lax.axis_size("cores"), lax.axis_size("block")
    group, row = lax.axis_index("groups"), lax.axis_index("dp")
    pieces = owner_slot.shape[0]
    per_row, features, width = basis_store.shape
    part_features = features // groups

    flat_grads = gradients.reshape(slots, features)

    def share(index):
        return lax.dynamic_slice_in_dim(flat_grads, index * part_features, part_features, 1)

    rows = [share(group)]
    for step in range(1, groups):
        rows.append(shift(share((group + step) % groups), "groups", step))
    rows = jnp.concatenate(rows, axis=0)

    flat_acts = activations.reshape(slots, activations.shape[2])
    partial_act = lax.dot_general(
        basis_act, flat_acts, (((0,), (1,)), ((), ())), preferred_element_type=F32
    )
    window = partial_act.shape[0]
    act = reduce_scatter(partial_act.reshape(cores, window // cores, slots), "cores")
    act = reduce_scatter(act.reshape(blocks, -1, slots), "block").astype(BF16)
    act = gather(act, "block").reshape(-1, slots)
    act_rot_t = gather(act, "cores").reshape(window, slots)

    held = lax.dynamic_slice_in_dim(basis_store, group * part_features, part_features, 1)
    piece_of_slot = jnp.zeros((pieces,), jnp.int32).at[owner_slot].set(
        jnp.arange(pieces, dtype=jnp.int32)
    )
    totals = jnp.zeros((pieces, groups * slots, width), F32)
    for step in range(dp):
        source = (row - step) % dp
        for local in range(per_row):
            term = jnp.dot(rows, held[local], preferred_element_type=F32)
            index = piece_of_slot[source * per_row + local]
            totals = lax.dynamic_update_index_in_dim(totals, term, index, 0)
        if step < dp - 1:
            held = shift(held, "dp", 1)

    by_block = totals.reshape(blocks, cores, groups, slots, width)
    mine = reduce_scatter(jnp.moveaxis(by_block, 1, 0), "cores")
    mine = reduce_scatter(mine, "block")
    total = mine[0]
    for step in range(1, groups):
        total = total + shift(mine[step], "groups", -step)
    positions = jnp.arange(LEN, dtype=jnp.int32)
    in_range = (positions[None, :] < token_counts[:, None]).astype(F32)
    grad_rot = total.reshape(seq_local, LEN, width) * in_range[:, :, None]
    grad_rot = grad_rot.astype(BF16)

    wanted = reader_blocks[0]
    chosen = jnp.concatenate(
        [
            lax.dynamic_slice_in_dim(act_rot_t, wanted[r] * BW, BW, 0)
            for r in range(wanted.shape[0])
        ],
        axis=0,
    )
    chosen = chosen.reshape(-1, seq_local, LEN)
    products = jnp.einsum("rsl,slc->src", chosen, grad_rot, preferred_element_type=F32)
    partial_sq = jnp.sum(products * products, axis=0)
    summed = reduce_scatter(partial_sq.reshape(dp, -1, width), "dp", BF16)
    return summed / (seq_local * dp)


def solution(mesh):
    in_specs = (
        P(("groups", "dp"), None, ("block", "cores")),
        P(("groups", "dp"), None, ("block", "cores")),
        P(("groups", "dp")),
        P(("block", "cores"), None),
        P("dp", ("block", "cores"), None),
        P(),
        P(("block", "cores"), None),
    )
    out_specs = P(("groups", "dp"), ("block", "cores"))
    return jax.shard_map(
        on_device, mesh=mesh, in_specs=in_specs, out_specs=out_specs, check_vma=False
    )
```

```python
import jax
import jax.numpy as jnp
from jax import lax
from jax.sharding import PartitionSpec as P

BW = 512
LEN = 128
F32 = jnp.float32
BF16 = jnp.bfloat16


def shift(value, axis, step):
    size = lax.axis_size(axis)
    return lax.ppermute(value, axis, [(i, (i + step) % size) for i in range(size)])


def block_of(value, index):
    return lax.dynamic_index_in_dim(value, index, 0, keepdims=False)


def reduce_scatter(blocks, axis, wire=F32):
    size, me = lax.axis_size(axis), lax.axis_index(axis)
    total = block_of(blocks, me)
    for step in range(1, size):
        term = block_of(blocks, (me + step) % size).astype(wire)
        total = total + shift(term, axis, step).astype(F32)
    return total


def gather(block, axis):
    size, me = lax.axis_size(axis), lax.axis_index(axis)
    out = jnp.zeros((size,) + block.shape, block.dtype)
    out = lax.dynamic_update_index_in_dim(out, block, me, 0)
    for step in range(1, size):
        came = shift(block, axis, step)
        out = lax.dynamic_update_index_in_dim(out, came, (me - step) % size, 0)
    return out


def on_device(
    activations, gradients, token_counts, basis_act, basis_store, owner_slot, reader_blocks
):
    seq_local = activations.shape[0]
    slots = seq_local * LEN
    groups, dp = lax.axis_size("groups"), lax.axis_size("dp")
    cores, blocks = lax.axis_size("cores"), lax.axis_size("block")
    group, row = lax.axis_index("groups"), lax.axis_index("dp")
    pieces = owner_slot.shape[0]
    per_row, features, width = basis_store.shape
    part_features = features // groups

    flat_grads = gradients.reshape(slots, features)

    def share(index):
        return lax.dynamic_slice_in_dim(flat_grads, index * part_features, part_features, 1)

    rows = [share(group)]
    for step in range(1, groups):
        rows.append(shift(share((group + step) % groups), "groups", step))
    rows = jnp.concatenate(rows, axis=0)

    flat_acts = activations.reshape(slots, activations.shape[2])
    partial_act = lax.dot_general(
        basis_act, flat_acts, (((0,), (1,)), ((), ())), preferred_element_type=F32
    )
    window = partial_act.shape[0]
    act = reduce_scatter(partial_act.reshape(cores, window // cores, slots), "cores")
    act = reduce_scatter(act.reshape(blocks, -1, slots), "block").astype(BF16)
    act = gather(act, "block").reshape(-1, slots)
    act_rot_t = gather(act, "cores").reshape(window, slots)

    held = lax.dynamic_slice_in_dim(basis_store, group * part_features, part_features, 1)
    piece_of_slot = jnp.zeros((pieces,), jnp.int32).at[owner_slot].set(
        jnp.arange(pieces, dtype=jnp.int32)
    )
    totals = jnp.zeros((pieces, groups * slots, width), F32)
    for step in range(dp):
        source = (row - step) % dp
        for local in range(per_row):
            term = jnp.dot(rows, held[local], preferred_element_type=F32)
            index = piece_of_slot[source * per_row + local]
            totals = lax.dynamic_update_index_in_dim(totals, term, index, 0)
        if step < dp - 1:
            if step == dp - 2:
                held, act_rot_t = lax.optimization_barrier((held, act_rot_t))
            held = shift(held, "dp", 1)

    by_block = totals.reshape(blocks, cores, groups, slots, width)
    mine = reduce_scatter(jnp.moveaxis(by_block, 1, 0), "cores")
    block = lax.axis_index("block")
    total = block_of(mine, block)[0]
    for far in range(blocks):
        toward = block_of(mine, (block + far) % blocks)
        for back in range(groups):
            if far or back:
                pairs = [
                    (g * blocks + b, ((g - back) % groups) * blocks + (b + far) % blocks)
                    for g in range(groups)
                    for b in range(blocks)
                ]
                total = total + lax.ppermute(toward[back], ("groups", "block"), pairs)
    positions = jnp.arange(LEN, dtype=jnp.int32)
    in_range = (positions[None, :] < token_counts[:, None]).astype(F32)
    grad_rot = total.reshape(seq_local, LEN, width) * in_range[:, :, None]
    grad_rot = grad_rot.astype(BF16)

    wanted = reader_blocks[0]
    chosen = jnp.concatenate(
        [
            lax.dynamic_slice_in_dim(act_rot_t, wanted[r] * BW, BW, 0)
            for r in range(wanted.shape[0])
        ],
        axis=0,
    )
    chosen = chosen.reshape(-1, seq_local, LEN)
    products = jnp.einsum("rsl,slc->src", chosen, grad_rot, preferred_element_type=F32)
    partial_sq = jnp.sum(products * products, axis=0)
    summed = reduce_scatter(partial_sq.reshape(dp, -1, width), "dp", BF16)
    return summed / (seq_local * dp)


def solution(mesh):
    in_specs = (
        P(("groups", "dp"), None, ("block", "cores")),
        P(("groups", "dp"), None, ("block", "cores")),
        P(("groups", "dp")),
        P(("block", "cores"), None),
        P("dp", ("block", "cores"), None),
        P(),
        P(("block", "cores"), None),
    )
    out_specs = P(("groups", "dp"), ("block", "cores"))
    return jax.shard_map(
        on_device, mesh=mesh, in_specs=in_specs, out_specs=out_specs, check_vma=False
    )
```

```python
import functools

import jax
import jax.numpy as jnp
from jax import lax
from jax.experimental import pallas as pl
from jax.experimental.pallas import tpu as pltpu
from jax.sharding import PartitionSpec as P

BW = 512
LEN = 128
F32 = jnp.float32
BF16 = jnp.bfloat16
VMEM_LIMIT = 40 * 1024 * 1024
VMEM = pl.BlockSpec(memory_space=pltpu.VMEM)
SMEM = pl.BlockSpec(memory_space=pltpu.SMEM)


def shift(value, axis, step):
    size = lax.axis_size(axis)
    return lax.ppermute(value, axis, [(i, (i + step) % size) for i in range(size)])


def block_of(value, index):
    return lax.dynamic_index_in_dim(value, index, 0, keepdims=False)


def reduce_scatter(blocks, axis):
    size, me = lax.axis_size(axis), lax.axis_index(axis)
    total = block_of(blocks, me)
    for step in range(1, size):
        total = total + shift(block_of(blocks, (me + step) % size), axis, step)
    return total


def gather(block, axis):
    size, me = lax.axis_size(axis), lax.axis_index(axis)
    out = jnp.zeros((size,) + block.shape, block.dtype)
    out = lax.dynamic_update_index_in_dim(out, block, me, 0)
    for step in range(1, size):
        came = shift(block, axis, step)
        out = lax.dynamic_update_index_in_dim(out, came, (me - step) % size, 0)
    return out


def rotate_kernel(cores, place, acts, basis, keep, send):
    height = keep.shape[0]
    for step in range(cores):
        share = lax.rem(place[1] + step, cores)
        columns = pl.ds(pl.multiple_of(share * height, height), height)
        term = jnp.dot(acts[...], basis[:, columns], preferred_element_type=F32)
        if step == 0:
            keep[...] = term.T
        else:
            send[step - 1] = term.T


def rotate(place, acts, basis, cores):
    height, width = basis.shape[1] // cores, acts.shape[0]
    return pl.pallas_call(
        functools.partial(rotate_kernel, cores),
        out_shape=(
            jax.ShapeDtypeStruct((height, width), F32),
            jax.ShapeDtypeStruct((cores - 1, height, width), F32),
        ),
        in_specs=[SMEM, VMEM, VMEM],
        out_specs=(VMEM, VMEM),
        compiler_params=pltpu.CompilerParams(vmem_limit_bytes=VMEM_LIMIT),
    )(place, acts, basis)


def pack_kernel(dp, cores, owner, place, rows, held, early, keep, send, last):
    row, core = place[0], place[1]
    last[...] = jnp.dot(rows[...], held[...], preferred_element_type=F32)
    for block in range(keep.shape[0]):
        for step in range(cores):
            piece = block * cores + lax.rem(core + step, cores)
            position = lax.rem(row - owner[piece] + dp, dp)
            target = keep.at[block] if step == 0 else send.at[step - 1, block]

            @pl.when(position == dp - 1)
            def _():
                target[...] = last[...]

            @pl.when(position < dp - 1)
            def _():
                target[...] = early[position]


def pack(owner_slot, place, rows, held, early, blocks, cores, dp):
    shape = (rows.shape[0], held.shape[1])
    return pl.pallas_call(
        functools.partial(pack_kernel, dp, cores),
        out_shape=(
            jax.ShapeDtypeStruct((blocks,) + shape, F32),
            jax.ShapeDtypeStruct((cores - 1, blocks) + shape, F32),
        ),
        in_specs=[SMEM, SMEM, VMEM, VMEM, VMEM],
        out_specs=(VMEM, VMEM),
        scratch_shapes=[pltpu.VMEM(shape, F32)],
        compiler_params=pltpu.CompilerParams(vmem_limit_bytes=VMEM_LIMIT),
    )(owner_slot, place, rows, held, early)


def square_kernel(dp, terms, counts, wanted, place, act, *refs):
    parts, outs = refs[:terms], refs[terms:]
    row = place[0]
    total = parts[0][...]
    for part in parts[1:]:
        total = total + part[...]
    sequences = total.shape[0] // LEN
    rotated = []
    for s in range(sequences):
        position = lax.broadcasted_iota(jnp.int32, (LEN, total.shape[1]), 0)
        used = jnp.where(position < counts[s], total[s * LEN : (s + 1) * LEN], 0.0)
        rotated.append(used.astype(BF16))
    height = outs[0].shape[0]
    for step in range(dp):
        start = lax.rem(row + step, dp) * height
        first = wanted[0, start // BW] * BW + lax.rem(start, BW)
        rows = pl.ds(pl.multiple_of(first, height), height)
        square = None
        for s in range(sequences):
            product = jnp.dot(
                act[rows, s * LEN : (s + 1) * LEN], rotated[s], preferred_element_type=F32
            )
            square = product * product if square is None else square + product * product
        outs[step][...] = square.astype(outs[step].dtype)


def squares(counts, wanted, place, act, parts, height, dp):
    width = parts[0].shape[1]
    return pl.pallas_call(
        functools.partial(square_kernel, dp, len(parts)),
        out_shape=tuple(
            jax.ShapeDtypeStruct((height, width), F32 if step == 0 else BF16)
            for step in range(dp)
        ),
        in_specs=[SMEM, SMEM, SMEM, VMEM] + [VMEM] * len(parts),
        out_specs=(VMEM,) * dp,
        compiler_params=pltpu.CompilerParams(vmem_limit_bytes=VMEM_LIMIT),
    )(counts, wanted, place, act, *parts)


def on_device(
    activations, gradients, token_counts, basis_act, basis_store, owner_slot, reader_blocks
):
    seq_local = activations.shape[0]
    slots = seq_local * LEN
    groups, dp = lax.axis_size("groups"), lax.axis_size("dp")
    cores, blocks = lax.axis_size("cores"), lax.axis_size("block")
    group, row = lax.axis_index("groups"), lax.axis_index("dp")
    block, core = lax.axis_index("block"), lax.axis_index("cores")
    _, features, width = basis_store.shape
    part_features = features // groups
    place = jnp.stack([row, core])

    held = lax.dynamic_slice_in_dim(basis_store[0], group * part_features, part_features, 0)
    flat_grads = gradients.reshape(slots, features)

    def share(index):
        return lax.dynamic_slice_in_dim(flat_grads, index * part_features, part_features, 1)

    away = [share((group + step) % groups) for step in range(1, groups)]
    pieces = [held]
    for step in range(1, dp):
        pieces.append(shift(pieces[-1], "dp", 1))
        if step == 1:
            pieces[1], activations = lax.optimization_barrier((pieces[1], activations))
    rows = [share(group)]
    for step in range(1, groups):
        rows.append(shift(away[step - 1], "groups", step))
    rows = jnp.concatenate(rows, axis=0)

    flat_acts = activations.reshape(slots, activations.shape[2])
    window = basis_act.shape[1]
    act, away = rotate(place, flat_acts, basis_act, cores)
    for step in range(1, cores):
        act = act + shift(away[step - 1], "cores", step)
    act = reduce_scatter(act.reshape(blocks, -1, slots), "block").astype(BF16)
    act = gather(act, "block").reshape(-1, slots)
    act_rot_t = gather(act, "cores").reshape(window, slots)

    early = [jnp.dot(rows, piece, preferred_element_type=F32) for piece in pieces[:-1]]
    held, act_rot_t = lax.optimization_barrier((pieces[-1], act_rot_t))
    keep, send = pack(
        owner_slot, place, rows, held, jnp.stack(early), blocks, cores, dp
    )
    for step in range(1, cores):
        keep = keep + shift(send[step - 1], "cores", step)

    mine = keep.reshape(blocks, groups, slots, width)
    parts = [block_of(mine, block)[0]]
    for far in range(blocks):
        toward = block_of(mine, (block + far) % blocks)
        for back in range(groups):
            if far or back:
                pairs = [
                    (g * blocks + b, ((g - back) % groups) * blocks + (b + far) % blocks)
                    for g in range(groups)
                    for b in range(blocks)
                ]
                parts.append(lax.ppermute(toward[back], ("groups", "block"), pairs))

    height = reader_blocks.shape[1] * BW // dp
    own, *others = squares(
        token_counts, reader_blocks, place, act_rot_t, parts, height, dp
    )
    for step in range(1, dp):
        own = own + shift(others[step - 1], "dp", step).astype(F32)
    return own / (seq_local * dp)


def solution(mesh):
    in_specs = (
        P(("groups", "dp"), None, ("block", "cores")),
        P(("groups", "dp"), None, ("block", "cores")),
        P(("groups", "dp")),
        P(("block", "cores"), None),
        P("dp", ("block", "cores"), None),
        P(),
        P(("block", "cores"), None),
    )
    out_specs = P(("groups", "dp"), ("block", "cores"))
    return jax.shard_map(
        on_device, mesh=mesh, in_specs=in_specs, out_specs=out_specs, check_vma=False
    )
```

```python
import functools

import jax
import jax.numpy as jnp
from jax import lax
from jax.experimental import pallas as pl
from jax.experimental.pallas import tpu as pltpu
from jax.sharding import PartitionSpec as P

BW = 512
LEN = 128
LINE = 4
F32 = jnp.float32
BF16 = jnp.bfloat16
VMEM_LIMIT = 40 * 1024 * 1024
VMEM = pl.BlockSpec(memory_space=pltpu.VMEM)
SMEM = pl.BlockSpec(memory_space=pltpu.SMEM)


def after(value, *gates):
    return lax.optimization_barrier((value,) + gates)[0]


def shift(value, axis, step):
    size = lax.axis_size(axis)
    return lax.ppermute(value, axis, [(i, (i + step) % size) for i in range(size)])


def block_of(value, index):
    return lax.dynamic_index_in_dim(value, index, 0, keepdims=False)


def reduce_scatter(blocks, axis):
    size, me = lax.axis_size(axis), lax.axis_index(axis)
    total = block_of(blocks, me)
    for step in range(1, size):
        total = total + shift(block_of(blocks, (me + step) % size), axis, step)
    return total


def gather(block, axis):
    size, me = lax.axis_size(axis), lax.axis_index(axis)
    out = jnp.zeros((size,) + block.shape, block.dtype)
    out = lax.dynamic_update_index_in_dim(out, block, me, 0)
    for step in range(1, size):
        came = shift(block, axis, step)
        out = lax.dynamic_update_index_in_dim(out, came, (me - step) % size, 0)
    return out


def rotate_kernel(cores, place, acts, basis, keep, send):
    height = keep.shape[0]
    for step in range(cores):
        share = lax.rem(place[1] + step, cores)
        columns = pl.ds(pl.multiple_of(share * height, height), height)
        term = jnp.dot(acts[...], basis[:, columns], preferred_element_type=F32)
        if step == 0:
            keep[...] = term.T
        else:
            send[step - 1] = term.T


def rotate(place, acts, basis, cores):
    height, width = basis.shape[1] // cores, acts.shape[0]
    return pl.pallas_call(
        functools.partial(rotate_kernel, cores),
        out_shape=(
            jax.ShapeDtypeStruct((height, width), F32),
            jax.ShapeDtypeStruct((cores - 1, height, width), F32),
        ),
        in_specs=[SMEM, VMEM, VMEM],
        out_specs=(VMEM, VMEM),
        compiler_params=pltpu.CompilerParams(vmem_limit_bytes=VMEM_LIMIT),
    )(place, acts, basis)


def is_middle(row):
    return jnp.logical_or(row == 1, row == 2)


def position_of(slot, row, dp):
    if dp != LINE:
        return lax.rem(row - slot + dp, dp)
    partner = row + 1 - 2 * lax.rem(row, 2)
    far = jnp.where(is_middle(slot), 2, 3)
    return jnp.where(slot == row, 0, jnp.where(slot == partner, 1, far))


def store_totals(dp, cores, owner, place, keep, send, store):
    row, core = place[0], place[1]
    for block in range(keep.shape[0]):
        for step in range(cores):
            piece = block * cores + lax.rem(core + step, cores)
            target = keep.at[block] if step == 0 else send.at[step - 1, block]
            store(position_of(owner[piece], row, dp), target)


def pack_shapes(blocks, cores, shape):
    return (
        jax.ShapeDtypeStruct((blocks,) + shape, F32),
        jax.ShapeDtypeStruct((cores - 1, blocks) + shape, F32),
    )


def pack_kernel(dp, cores, owner, place, rows, held, early, keep, send, last):
    last[...] = jnp.dot(rows[...], held[...], preferred_element_type=F32)

    def store(position, target):
        @pl.when(position == dp - 1)
        def _():
            target[...] = last[...]

        @pl.when(position < dp - 1)
        def _():
            target[...] = early[position]

    store_totals(dp, cores, owner, place, keep, send, store)


def pack(owner_slot, place, rows, held, early, blocks, cores, dp):
    shape = (rows.shape[0], held.shape[1])
    return pl.pallas_call(
        functools.partial(pack_kernel, dp, cores),
        out_shape=pack_shapes(blocks, cores, shape),
        in_specs=[SMEM, SMEM, VMEM, VMEM, VMEM],
        out_specs=(VMEM, VMEM),
        scratch_shapes=[pltpu.VMEM(shape, F32)],
        compiler_params=pltpu.CompilerParams(vmem_limit_bytes=VMEM_LIMIT),
    )(owner_slot, place, rows, held, early)


def multiply(target, rows, pieces):
    stops = [sum(part.shape[1] for part in rows[: i + 1]) for i in range(len(rows))]
    ends = [sum(part.shape[0] for part in pieces[: i + 1]) for i in range(len(pieces))]
    total, start = None, 0
    for stop in sorted(set(stops + ends)):
        i = [stop <= end for end in stops].index(True)
        j = [stop <= end for end in ends].index(True)
        left = start - stops[i] + rows[i].shape[1]
        top = start - ends[j] + pieces[j].shape[0]
        size = stop - start
        term = jnp.dot(
            rows[i][:, left : left + size],
            pieces[j][top : top + size],
            preferred_element_type=F32,
        )
        total, start = term if total is None else total + term, stop
    target[...] = total


def early_kernel(place, own, near, middle, end, *refs):
    rows, out = refs[:-1], refs[-1]
    multiply(out.at[0], rows, (own,))
    multiply(out.at[1], rows, (near,))

    @pl.when(is_middle(place[0]))
    def _():
        multiply(out.at[2], rows, (middle,))

    @pl.when(jnp.logical_not(is_middle(place[0])))
    def _():
        multiply(out.at[2], rows, (end,))


def early_products(place, rows, own, near, middle, end):
    shape = (3, rows[0].shape[0], own.shape[1])
    return pl.pallas_call(
        early_kernel,
        out_shape=jax.ShapeDtypeStruct(shape, F32),
        in_specs=[SMEM] + [VMEM] * (4 + len(rows)),
        out_specs=VMEM,
        compiler_params=pltpu.CompilerParams(vmem_limit_bytes=VMEM_LIMIT),
    )(place, own, near, middle, end, *rows)


def spare_kernel(
    cores, owner, place, mine, other, end_mine, end_other, own, near, far, out, keep, send, totals
):
    pieces, height = (own, near, far.at[0], far.at[1]), mine.shape[0]
    for position, piece in enumerate(pieces):
        for half, rows in enumerate((mine, other)):
            multiply(out.at[position, pl.ds(half * height, height)], (rows,), (piece,))
        for half, rows in enumerate((end_mine, end_other)):
            multiply(totals.at[position, pl.ds(half * height, height)], (rows,), (piece,))

    @pl.when(jnp.logical_not(is_middle(place[0])))
    def _():
        out[...] = jnp.zeros_like(out)

    def store(position, target):
        target[...] = totals[position]

    store_totals(LINE, cores, owner, place, keep, send, store)


def spare_products(owner_slot, place, rows, end_rows, own, near, far, blocks, cores):
    shape = (2 * rows[0].shape[0], own.shape[1])
    return pl.pallas_call(
        functools.partial(spare_kernel, cores),
        out_shape=(jax.ShapeDtypeStruct((LINE,) + shape, F32),)
        + pack_shapes(blocks, cores, shape),
        in_specs=[SMEM, SMEM] + [VMEM] * 7,
        out_specs=(VMEM,) * 3,
        scratch_shapes=[pltpu.VMEM((LINE,) + shape, F32)],
        compiler_params=pltpu.CompilerParams(vmem_limit_bytes=VMEM_LIMIT),
    )(owner_slot, place, *rows, *end_rows, own, near, far)


def late_kernel(
    cores, owner, place, mine, middle, end, end_rest, early_mine, early_other, spare, *refs
):
    other, (keep, send, last) = refs[:-3], refs[-3:]
    height = mine.shape[0]
    halves = (pl.ds(0, height), pl.ds(height, height))

    def products(*pieces):
        multiply(last.at[halves[0]], (mine,), pieces)
        multiply(last.at[halves[1]], other, pieces)

    @pl.when(is_middle(place[0]))
    def _():
        products(middle)

    @pl.when(jnp.logical_not(is_middle(place[0])))
    def _():
        products(end, end_rest)

    def store(position, target):
        @pl.when(position == LINE - 1)
        def _():
            target[...] = last[...] + spare[LINE - 1]

        @pl.when(position < LINE - 1)
        def _():
            for half, early in zip(halves, (early_mine, early_other)):
                target[half] = early[position] + spare[position, half]

    store_totals(LINE, cores, owner, place, keep, send, store)


def late_products(owner_slot, place, mine, other, middle, ends, early, spare, blocks, cores):
    shape = (2 * mine.shape[0], middle.shape[1])
    return pl.pallas_call(
        functools.partial(late_kernel, cores),
        out_shape=pack_shapes(blocks, cores, shape),
        in_specs=[SMEM, SMEM] + [VMEM] * (7 + len(other)),
        out_specs=(VMEM, VMEM),
        scratch_shapes=[pltpu.VMEM(shape, F32)],
        compiler_params=pltpu.CompilerParams(vmem_limit_bytes=VMEM_LIMIT),
    )(owner_slot, place, mine, middle, *ends, *early, spare, *other)


def square_kernel(dp, terms, counts, wanted, place, act, *refs):
    parts, outs = refs[:terms], refs[terms:]
    row = place[0]
    total = parts[0][...]
    for part in parts[1:]:
        total = total + part[...]
    sequences = total.shape[0] // LEN
    rotated = []
    for s in range(sequences):
        position = lax.broadcasted_iota(jnp.int32, (LEN, total.shape[1]), 0)
        used = jnp.where(position < counts[s], total[s * LEN : (s + 1) * LEN], 0.0)
        rotated.append(used.astype(BF16))
    height = outs[0].shape[0]
    for step in range(dp):
        start = lax.rem(row + step, dp) * height
        first = wanted[0, start // BW] * BW + lax.rem(start, BW)
        rows = pl.ds(pl.multiple_of(first, height), height)
        square = None
        for s in range(sequences):
            product = jnp.dot(
                act[rows, s * LEN : (s + 1) * LEN], rotated[s], preferred_element_type=F32
            )
            square = product * product if square is None else square + product * product
        outs[step][...] = square.astype(outs[step].dtype)


def squares(counts, wanted, place, act, parts, height, dp):
    width = parts[0].shape[1]
    return pl.pallas_call(
        functools.partial(square_kernel, dp, len(parts)),
        out_shape=tuple(
            jax.ShapeDtypeStruct((height, width), F32 if step == 0 else BF16)
            for step in range(dp)
        ),
        in_specs=[SMEM, SMEM, SMEM, VMEM] + [VMEM] * len(parts),
        out_specs=(VMEM,) * dp,
        compiler_params=pltpu.CompilerParams(vmem_limit_bytes=VMEM_LIMIT),
    )(counts, wanted, place, act, *parts)


def along(value, pairs):
    return lax.ppermute(value, "dp", pairs)


def across(value, group_step, pairs):
    groups, dp = lax.axis_size("groups"), lax.axis_size("dp")
    full = [
        (g * dp + here, (g + group_step) % groups * dp + there)
        for g in range(groups)
        for here, there in pairs
    ]
    return lax.ppermute(value, ("groups", "dp"), full)


def exchange(keep, groups, rows=None):
    blocks, block = lax.axis_size("block"), lax.axis_index("block")
    dp = lax.axis_size("dp")
    rows = range(dp) if rows is None else rows
    mine = keep.reshape(blocks, groups, -1, keep.shape[-1])
    parts = [block_of(mine, block)[0]]
    for far in range(blocks):
        toward = block_of(mine, (block + far) % blocks)
        for back in range(groups):
            if far or back:
                pairs = [
                    (
                        (g * dp + row) * blocks + b,
                        ((g - back) % groups * dp + row) * blocks + (b + far) % blocks,
                    )
                    for g in range(groups)
                    for row in rows
                    for b in range(blocks)
                ]
                parts.append(lax.ppermute(toward[back], ("groups", "dp", "block"), pairs))
    return parts


def swap_cores(keep, send, rows=None):
    cores, dp = lax.axis_size("cores"), lax.axis_size("dp")
    rows = range(dp) if rows is None else rows
    for step in range(1, cores):
        pairs = [
            (row * cores + core, row * cores + (core + step) % cores)
            for row in rows
            for core in range(cores)
        ]
        keep = keep + lax.ppermute(send[step - 1], ("dp", "cores"), pairs)
    return keep


def scatter_act(act):
    blocks = lax.axis_size("block")
    return reduce_scatter(act.reshape(blocks, -1, act.shape[-1]), "block").astype(BF16)


def gather_act(act):
    cores, blocks = lax.axis_size("cores"), lax.axis_size("block")
    core, block = lax.axis_index("cores"), lax.axis_index("block")
    out = jnp.zeros((cores, blocks) + act.shape, act.dtype)
    for far in range(blocks):
        for step in range(cores):
            came = act
            if far or step:
                pairs = [
                    (b * cores + c, (b + far) % blocks * cores + (c + step) % cores)
                    for b in range(blocks)
                    for c in range(cores)
                ]
                came = lax.ppermute(act, ("block", "cores"), pairs)
            source = ((core - step) % cores, (block - far) % blocks, 0, 0)
            out = lax.dynamic_update_slice(out, came[None, None], source)
    return out.reshape(-1, act.shape[-1])


def ring_terms(place, activations, gradients, basis_act, piece, owner_slot, group_slice):
    groups, dp = lax.axis_size("groups"), lax.axis_size("dp")
    cores, blocks = lax.axis_size("cores"), lax.axis_size("block")
    size = piece.shape[0] // groups
    pieces = [group_slice(piece, 0, 0, size, 0)]
    for step in range(1, dp):
        pieces.append(shift(pieces[-1], "dp", 1))
    act, away = rotate(place, activations.reshape(-1, activations.shape[-1]), basis_act, cores)
    act = scatter_act(swap_cores(act, away))
    act = gather(act, "block").reshape(-1, act.shape[-1])
    act = gather(act, "cores").reshape(-1, act.shape[-1])
    rows = [group_slice(gradients, 0, 0, size, 1)]
    for step in range(1, groups):
        rows.append(shift(group_slice(gradients, step, 0, size, 1), "groups", step))
    rows = jnp.concatenate(rows, axis=0)
    early = [jnp.dot(rows, held, preferred_element_type=F32) for held in pieces[:-1]]
    last, act = lax.optimization_barrier((pieces[-1], act))
    keep, send = pack(owner_slot, place, rows, last, jnp.stack(early), blocks, cores, dp)
    return exchange(swap_cores(keep, send), groups), act


def line_terms(place, activations, gradients, basis_act, piece, owner_slot, group_slice):
    cores, blocks = lax.axis_size("cores"), lax.axis_size("block")
    size = piece.shape[0] // 2
    spare = size * 2 // 9 // 128 * 128
    main = size - spare
    inner = [(1, 2), (2, 1)]
    outward = [(1, 0), (2, 3)]
    inward = [(0, 1), (3, 2)]
    neighbours = inward + outward
    every = [(i, i) for i in range(LINE)]

    own = group_slice(piece, 0, 0, main, 0)
    near = along(own, neighbours)
    middle = along(own, inner)
    gradients = after(gradients, own)
    mine = group_slice(gradients, 0, 0, main, 1)
    mine_spare = group_slice(gradients, 0, main, spare, 1)
    cuts = (0, main // 4 // 128 * 128, main * 2 // 3 // 128 * 128, main)
    away = [
        group_slice(gradients, 1, start, stop - start, 1)
        for start, stop in zip(cuts[:-1], cuts[1:])
    ]
    other_spare = across(group_slice(gradients, 1, main, spare, 1), 1, every)
    other = [across(away[0], 1, every)]
    own_spare = group_slice(piece, 0, main, spare, 0)
    act, act_away = rotate(
        place, activations.reshape(-1, activations.shape[-1]), basis_act, cores
    )

    (
        near, middle, own_spare, mine_spare, other_spare, other[0], away[1], away[2], act, act_away
    ) = lax.optimization_barrier(
        (near, middle, own_spare, mine_spare, other_spare, other[0], away[1], away[2], act, act_away)
    )
    height, width = mine.shape[0], own.shape[1]
    folds = spare // height
    far = along(near, inner)
    end_third = along(middle, outward)
    folded = [own_spare[i * height : (i + 1) * height] for i in range(folds)]
    arrived = along(jnp.concatenate([mine_spare] + folded, axis=1), inward)
    other.append(across(away[1], 1, every))
    act = scatter_act(swap_cores(act, act_away))

    far, end_third, arrived, other[1], act, other_spare, away[2] = lax.optimization_barrier(
        (far, end_third, arrived, other[1], act, other_spare, away[2])
    )
    end_mine = arrived[:, :spare]
    near_spare = jnp.concatenate(
        [arrived[:, spare + i * width : spare + (i + 1) * width] for i in range(folds)], axis=0
    )
    half = main * 4 // 7 // 128 * 128
    end_last = along(far[:half], outward)
    far_spare = along(jnp.stack([own_spare, near_spare]), inner)
    end_other = along(other_spare, inward)
    other.append(across(away[2], 1, every))
    act = gather_act(act)
    early_mine = early_products(place, [mine], own, near, middle, end_third)

    rest, end_last, far_spare, end_other, other[2], early_mine = lax.optimization_barrier(
        (far[half:], end_last, far_spare, end_other, other[2], early_mine)
    )
    end_rest = along(rest, outward)
    early_other = early_products(place, other, own, near, middle, end_third)
    spare_totals, keep, send = spare_products(
        owner_slot,
        place,
        (mine_spare, other_spare),
        (end_mine, end_other),
        own_spare,
        near_spare,
        far_spare,
        blocks,
        cores,
    )
    for_end = exchange(swap_cores(keep, send, (1, 2)), 2, (1, 2))
    end_rest = after(end_rest, act, early_other, spare_totals)
    keep, send = late_products(
        owner_slot,
        place,
        mine,
        other,
        far,
        (end_last, end_rest),
        (early_mine, early_other),
        spare_totals,
        blocks,
        cores,
    )
    keep = swap_cores(keep, send)
    parts = exchange(keep, 2)
    total = after(for_end[0], keep)
    for part in for_end[1:]:
        total = total + part
    return parts + [along(total, outward)], act


def on_device(
    activations, gradients, token_counts, basis_act, basis_store, owner_slot, reader_blocks
):
    seq_local = activations.shape[0]
    groups, dp = lax.axis_size("groups"), lax.axis_size("dp")
    group, row = lax.axis_index("groups"), lax.axis_index("dp")
    place = jnp.stack([row, lax.axis_index("cores")])
    part_features = basis_store.shape[1] // groups

    def group_slice(value, step, start, size, axis):
        first = (group + step) % groups * part_features + start
        return lax.dynamic_slice_in_dim(value, first, size, axis)

    flat_grads = gradients.reshape(seq_local * LEN, -1)
    terms = line_terms if (dp, groups) == (LINE, 2) else ring_terms
    parts, act = terms(
        place, activations, flat_grads, basis_act, basis_store[0], owner_slot, group_slice
    )
    height = reader_blocks.shape[1] * BW // dp
    total, *others = squares(token_counts, reader_blocks, place, act, parts, height, dp)
    for step in range(1, dp):
        total = total + shift(others[step - 1], "dp", step).astype(F32)
    return total / (seq_local * dp)


def solution(mesh):
    in_specs = (
        P(("groups", "dp"), None, ("block", "cores")),
        P(("groups", "dp"), None, ("block", "cores")),
        P(("groups", "dp")),
        P(("block", "cores"), None),
        P("dp", ("block", "cores"), None),
        P(),
        P(("block", "cores"), None),
    )
    out_specs = P(("groups", "dp"), ("block", "cores"))
    return jax.shard_map(
        on_device, mesh=mesh, in_specs=in_specs, out_specs=out_specs, check_vma=False
    )
```

```python
import functools

import jax
import jax.numpy as jnp
from jax import lax
from jax.experimental import pallas as pl
from jax.experimental.pallas import tpu as pltpu
from jax.sharding import PartitionSpec as P

BW = 512
LEN = 128
FLOPS_SCALE = 1
F32 = jnp.float32
BF16 = jnp.bfloat16
VMEM_LIMIT = 40 * 1024 * 1024
VMEM = pl.BlockSpec(memory_space=pltpu.VMEM)
SMEM = pl.BlockSpec(memory_space=pltpu.SMEM)


def after(value, *gates):
    return lax.optimization_barrier((value,) + gates)[0]


def shift(value, axis, step):
    size = lax.axis_size(axis)
    return lax.ppermute(value, axis, [(i, (i + step) % size) for i in range(size)])


def block_of(value, index):
    return lax.dynamic_index_in_dim(value, index, 0, keepdims=False)


def to_neighbour(value, far, step):
    cores, blocks = lax.axis_size("cores"), lax.axis_size("block")
    pairs = [
        (b * cores + c, (b + far) % blocks * cores + (c + step) % cores)
        for b in range(blocks)
        for c in range(cores)
    ]
    return lax.ppermute(value, ("block", "cores"), pairs)


def gather_act(act):
    cores, blocks = lax.axis_size("cores"), lax.axis_size("block")
    core, block = lax.axis_index("cores"), lax.axis_index("block")
    out = jnp.zeros((cores, blocks) + act.shape, act.dtype)
    for far in range(blocks):
        for step in range(cores):
            came = to_neighbour(act, far, step) if far or step else act
            source = ((core - step) % cores, (block - far) % blocks, 0, 0)
            out = lax.dynamic_update_slice(out, came[None, None], source)
    return out.reshape(-1, act.shape[-1])


def rotate_kernel(blocks, cores, place, acts, basis, *outs):
    height = outs[0].shape[0]
    for core_step in range(cores):
        core = lax.rem(place[1] + core_step, cores)
        span = blocks * height
        columns = pl.ds(pl.multiple_of(core * span, span), span)
        term = jnp.dot(acts[...], basis[:, columns], preferred_element_type=F32)
        for share in range(blocks):
            step = lax.rem(share - place[2] + blocks, blocks)
            part = term[:, share * height : (share + 1) * height].T
            for i in range(blocks):

                @pl.when(step == i)
                def _():
                    outs[i * cores + core_step][...] = part


def rotate(place, acts, basis, blocks, cores):
    shape = (basis.shape[1] // (blocks * cores), acts.shape[0])
    return pl.pallas_call(
        functools.partial(rotate_kernel, blocks, cores),
        out_shape=(jax.ShapeDtypeStruct(shape, F32),) * (blocks * cores),
        in_specs=[SMEM, VMEM, VMEM],
        out_specs=(VMEM,) * (blocks * cores),
        compiler_params=pltpu.CompilerParams(vmem_limit_bytes=VMEM_LIMIT),
    )(place, acts, basis)


def product(rows, piece, start):
    total, first = None, 0
    for part in rows:
        last = first + part.shape[1]
        low, high = max(first, start), min(last, start + piece.shape[0])
        if low < high:
            term = jnp.dot(
                part[:, low - first : high - first],
                piece[low - start : high - start],
                preferred_element_type=F32,
            )
            total = term if total is None else total + term
        first = last
    return total


def early_kernel(parts, shares, *refs):
    rows, pieces, out = refs[:parts], refs[parts:-1], refs[-1]
    for position in range(out.shape[0]):
        total = None
        for share, start in enumerate(shares):
            i = position * len(shares) + share
            if i < len(pieces):
                term = product(rows, pieces[i], start)
                total = term if total is None else total + term
        out[position] = total


def early_products(rows, pieces, shares):
    positions = -(-len(pieces) // len(shares))
    height, width = rows[0].shape[0], pieces[0].shape[1]
    flops = 2 * height * width * sum(piece.shape[0] for piece in pieces)
    return pl.pallas_call(
        functools.partial(early_kernel, len(rows), shares),
        out_shape=jax.ShapeDtypeStruct((positions, height, width), F32),
        in_specs=[VMEM] * (len(rows) + len(pieces)),
        out_specs=VMEM,
        compiler_params=pltpu.CompilerParams(vmem_limit_bytes=VMEM_LIMIT),
        cost_estimate=pl.CostEstimate(
            flops=FLOPS_SCALE * flops, bytes_accessed=flops // width, transcendentals=0
        ),
    )(*rows, *pieces)


def pack_kernel(dp, cores, parts, start, owner, place, held, *refs):
    row, core = place[0], place[1]
    groups, refs = len(parts), list(refs)
    rows = [[refs.pop(0) for _ in range(cuts)] for cuts in parts]
    early = [refs.pop(0) for _ in parts]
    almost = [refs.pop(0) for _ in parts]
    last, height = refs.pop(), early[0].shape[1]
    spans = [pl.ds(g * height, height) for g in range(groups)]
    for g in range(groups):
        last[spans[g]] = almost[g][0] + product(rows[g], held, start)
    for block in range(refs[0].shape[0]):
        for step in range(cores):
            piece = block * cores + lax.rem(core + step, cores)
            position = lax.rem(row - owner[piece] + dp, dp)
            target = refs[step].at[block]

            @pl.when(position == dp - 1)
            def _():
                target[...] = last[...]

            @pl.when(position < dp - 1)
            def _():
                for g in range(groups):
                    target[spans[g]] = early[g][position]


def pack(owner_slot, place, rows, held, start, early, almost, blocks, cores):
    positions, height, width = early[0].shape
    shape = (len(rows) * height, width)
    parts = tuple(len(part) for part in rows)
    return pl.pallas_call(
        functools.partial(pack_kernel, positions + 1, cores, parts, start),
        out_shape=(jax.ShapeDtypeStruct((blocks,) + shape, F32),) * cores,
        in_specs=[SMEM, SMEM] + [VMEM] * (1 + sum(parts) + 2 * len(rows)),
        out_specs=(VMEM,) * cores,
        scratch_shapes=[pltpu.VMEM(shape, F32)],
        compiler_params=pltpu.CompilerParams(vmem_limit_bytes=VMEM_LIMIT),
    )(owner_slot, place, held, *[cut for part in rows for cut in part], *early, *almost)


def square_kernel(dp, terms, counts, wanted, place, act, *refs):
    parts, outs = refs[:terms], refs[terms:]
    row = place[0]
    total = parts[0][...]
    for part in parts[1:]:
        total = total + part[...]
    sequences = total.shape[0] // LEN
    rotated = []
    for s in range(sequences):
        position = lax.broadcasted_iota(jnp.int32, (LEN, total.shape[1]), 0)
        used = jnp.where(position < counts[s], total[s * LEN : (s + 1) * LEN], 0.0)
        rotated.append(used.astype(BF16))
    height = outs[0].shape[0]
    for step in range(dp):
        start = lax.rem(row + step, dp) * height
        first = wanted[0, start // BW] * BW + lax.rem(start, BW)
        rows = pl.ds(pl.multiple_of(first, height), height)
        square = None
        for s in range(sequences):
            product = jnp.dot(
                act[rows, s * LEN : (s + 1) * LEN], rotated[s], preferred_element_type=F32
            )
            square = product * product if square is None else square + product * product
        outs[step][...] = square.astype(outs[step].dtype)


def squares(counts, wanted, place, act, parts, height, dp):
    width = parts[0].shape[1]
    return pl.pallas_call(
        functools.partial(square_kernel, dp, len(parts)),
        out_shape=tuple(
            jax.ShapeDtypeStruct((height, width), F32 if step == 0 else BF16)
            for step in range(dp)
        ),
        in_specs=[SMEM, SMEM, SMEM, VMEM] + [VMEM] * len(parts),
        out_specs=(VMEM,) * dp,
        compiler_params=pltpu.CompilerParams(vmem_limit_bytes=VMEM_LIMIT),
    )(counts, wanted, place, act, *parts)


def on_device(
    activations, gradients, token_counts, basis_act, basis_store, owner_slot, reader_blocks
):
    seq_local = activations.shape[0]
    slots = seq_local * LEN
    groups, dp = lax.axis_size("groups"), lax.axis_size("dp")
    cores, blocks = lax.axis_size("cores"), lax.axis_size("block")
    group, row = lax.axis_index("groups"), lax.axis_index("dp")
    block, core = lax.axis_index("block"), lax.axis_index("cores")
    _, features, width = basis_store.shape
    part_features = features // groups
    place = jnp.stack([row, core, block])

    cut = -(-part_features // 256) * 128
    shares = (0, cut)
    rings = [
        [lax.dynamic_slice_in_dim(basis_store[0], group * part_features + start, size, 0)]
        for start, size in zip(shares, (cut, part_features - cut))
    ]
    flat_grads = after(gradients.reshape(slots, features), rings[0][0], rings[1][0])

    def share(index, start, size):
        return lax.dynamic_slice_in_dim(flat_grads, index * part_features + start, size, 1)

    rows, first = [[share(group, 0, part_features)]], part_features * 7 // 10 // 128 * 128
    for step in range(1, groups):
        rows.append(
            [
                shift(share((group + step) % groups, start, size), "groups", step)
                for start, size in ((0, first), (first, part_features - first))
            ]
        )

    flat_acts = activations.reshape(slots, activations.shape[2])
    act, *away = rotate(place, flat_acts, basis_act, blocks, cores)
    for step in range(1, dp):
        for ring in rings:
            ring.append(shift(ring[-1], "dp", 1))
    away = [to_neighbour(part, i // cores, i % cores) for i, part in enumerate(away, 1)]
    for part in away:
        act = act + part
    act_rot_t = gather_act(act.astype(BF16))

    pieces = [ring[step] for step in range(dp) for ring in rings]
    early = [early_products(part, pieces[:-2], shares) for part in rows]
    almost = [early_products(part, pieces[-2:-1], shares[:1]) for part in rows]
    last, *almost = lax.optimization_barrier((pieces[-1], *almost))
    keep, *send = pack(
        owner_slot, place, rows, last, cut, early, almost, blocks, cores
    )
    for step in range(1, cores):
        keep = keep + shift(send[step - 1], "cores", step)
    keep, act_rot_t = lax.optimization_barrier((keep, act_rot_t))

    mine = keep.reshape(blocks, groups, slots, width)
    parts = [block_of(mine, block)[0]]
    for far in range(blocks):
        toward = block_of(mine, (block + far) % blocks)
        for back in range(groups):
            if far or back:
                pairs = [
                    (g * blocks + b, ((g - back) % groups) * blocks + (b + far) % blocks)
                    for g in range(groups)
                    for b in range(blocks)
                ]
                parts.append(lax.ppermute(toward[back], ("groups", "block"), pairs))

    height = reader_blocks.shape[1] * BW // dp
    own, *others = squares(
        token_counts, reader_blocks, place, act_rot_t, parts, height, dp
    )
    for step in range(1, dp):
        own = own + shift(others[step - 1], "dp", step).astype(F32)
    return own / (seq_local * dp)


def solution(mesh):
    in_specs = (
        P(("groups", "dp"), None, ("block", "cores")),
        P(("groups", "dp"), None, ("block", "cores")),
        P(("groups", "dp")),
        P(("block", "cores"), None),
        P("dp", ("block", "cores"), None),
        P(),
        P(("block", "cores"), None),
    )
    out_specs = P(("groups", "dp"), ("block", "cores"))
    return jax.shard_map(
        on_device, mesh=mesh, in_specs=in_specs, out_specs=out_specs, check_vma=False
    )
```

```python
import functools

import jax
import jax.numpy as jnp
from jax import lax
from jax.experimental import pallas as pl
from jax.experimental.pallas import tpu as pltpu
from jax.sharding import PartitionSpec as P

BW = 512
LEN = 128
FLOPS_SCALE = 1
F32 = jnp.float32
BF16 = jnp.bfloat16
VMEM_LIMIT = 40 * 1024 * 1024
VMEM = pl.BlockSpec(memory_space=pltpu.VMEM)
SMEM = pl.BlockSpec(memory_space=pltpu.SMEM)


def after(value, *gates):
    return lax.optimization_barrier((value,) + gates)[0]


def shift(value, axis, step):
    size = lax.axis_size(axis)
    return lax.ppermute(value, axis, [(i, (i + step) % size) for i in range(size)])


def block_of(value, index):
    return lax.dynamic_index_in_dim(value, index, 0, keepdims=False)


def to_neighbour(value, far, step):
    cores, blocks = lax.axis_size("cores"), lax.axis_size("block")
    pairs = [
        (b * cores + c, (b + far) % blocks * cores + (c + step) % cores)
        for b in range(blocks)
        for c in range(cores)
    ]
    return lax.ppermute(value, ("block", "cores"), pairs)


def gather_act(act):
    cores, blocks = lax.axis_size("cores"), lax.axis_size("block")
    core, block = lax.axis_index("cores"), lax.axis_index("block")
    out = jnp.zeros((cores, blocks) + act.shape, act.dtype)
    for far in range(blocks):
        for step in range(cores):
            came = to_neighbour(act, far, step) if far or step else act
            source = ((core - step) % cores, (block - far) % blocks, 0, 0)
            out = lax.dynamic_update_slice(out, came[None, None], source)
    return out.reshape(-1, act.shape[-1])


def rotate_kernel(blocks, cores, place, acts, basis, *outs):
    height = outs[0].shape[0]
    for core_step in range(cores):
        core = lax.rem(place[1] + core_step, cores)
        span = blocks * height
        columns = pl.ds(pl.multiple_of(core * span, span), span)
        term = jnp.dot(acts[...], basis[:, columns], preferred_element_type=F32)
        for share in range(blocks):
            step = lax.rem(share - place[2] + blocks, blocks)
            part = term[:, share * height : (share + 1) * height].T
            for i in range(blocks):

                @pl.when(step == i)
                def _():
                    outs[i * cores + core_step][...] = part


def rotate(place, acts, basis, blocks, cores):
    shape = (basis.shape[1] // (blocks * cores), acts.shape[0])
    return pl.pallas_call(
        functools.partial(rotate_kernel, blocks, cores),
        out_shape=(jax.ShapeDtypeStruct(shape, F32),) * (blocks * cores),
        in_specs=[SMEM, VMEM, VMEM],
        out_specs=(VMEM,) * (blocks * cores),
        compiler_params=pltpu.CompilerParams(vmem_limit_bytes=VMEM_LIMIT),
    )(place, acts, basis)


def product(rows, piece, start):
    total, first = None, 0
    for part in rows:
        last = first + part.shape[1]
        low, high = max(first, start), min(last, start + piece.shape[0])
        if low < high:
            term = jnp.dot(
                part[:, low - first : high - first],
                piece[low - start : high - start],
                preferred_element_type=F32,
            )
            total = term if total is None else total + term
        first = last
    return total


def early_kernel(parts, shares, *refs):
    rows, pieces, out = refs[:parts], refs[parts:-1], refs[-1]
    for position in range(out.shape[0]):
        total = None
        for share, start in enumerate(shares):
            i = position * len(shares) + share
            if i < len(pieces):
                term = product(rows, pieces[i], start)
                total = term if total is None else total + term
        out[position] = total


def early_products(rows, pieces, shares):
    positions = -(-len(pieces) // len(shares))
    height, width = rows[0].shape[0], pieces[0].shape[1]
    flops = 2 * height * width * sum(piece.shape[0] for piece in pieces)
    return pl.pallas_call(
        functools.partial(early_kernel, len(rows), shares),
        out_shape=jax.ShapeDtypeStruct((positions, height, width), F32),
        in_specs=[VMEM] * (len(rows) + len(pieces)),
        out_specs=VMEM,
        compiler_params=pltpu.CompilerParams(vmem_limit_bytes=VMEM_LIMIT),
        cost_estimate=pl.CostEstimate(
            flops=FLOPS_SCALE * flops, bytes_accessed=flops // width, transcendentals=0
        ),
    )(*rows, *pieces)


def total_of(position, early, last, group):
    positions = early[0].shape[0]
    height = early[0].shape[1]
    at_last = last[pl.ds(group * height, height)]
    before = early[group][jnp.minimum(position, positions - 1)]
    return jnp.where(position == positions, at_last, before)


def pack_kernel(dp, cores, parts, owner, place, held, *refs):
    row, core = place[0], place[1]
    refs = list(refs)
    rows = [[refs.pop(0) for _ in range(cuts)] for cuts in parts]
    early = [refs.pop(0) for _ in parts]
    last, sends = refs[0], refs[1:]
    height = early[0].shape[1]
    for g in range(len(parts)):
        last[g * height : (g + 1) * height] = product(rows[g], held, 0)
    for step in range(1, cores):
        for block in range(sends[0].shape[0]):
            piece = block * cores + lax.rem(core + step, cores)
            position = lax.rem(row - owner[piece] + dp, dp)
            for g in range(len(parts)):
                sends[step - 1][block, g * height : (g + 1) * height] = total_of(
                    position, early, last, g
                )


def pack(owner_slot, place, rows, held, early, blocks, cores):
    positions, height, width = early[0].shape
    shape = (len(rows) * height, width)
    parts = tuple(len(part) for part in rows)
    return pl.pallas_call(
        functools.partial(pack_kernel, positions + 1, cores, parts),
        out_shape=(jax.ShapeDtypeStruct(shape, F32),)
        + (jax.ShapeDtypeStruct((blocks,) + shape, F32),) * (cores - 1),
        in_specs=[SMEM, SMEM] + [VMEM] * (1 + sum(parts) + len(rows)),
        out_specs=(VMEM,) * cores,
        compiler_params=pltpu.CompilerParams(vmem_limit_bytes=VMEM_LIMIT),
    )(owner_slot, place, held, *[cut for part in rows for cut in part], *early)


def join_kernel(dp, cores, groups, blocks, owner, place, last, *refs):
    row, core, me = place[0], place[1], place[2]
    early, came, outs = refs[:groups], refs[groups : groups + cores - 1], refs[groups + cores - 1 :]
    height = early[0].shape[1]
    for far in range(blocks):
        block = lax.rem(me + far, blocks)
        position = lax.rem(row - owner[block * cores + core] + dp, dp)
        for g in range(groups):
            total = total_of(position, early, last, g)
            for other in came:
                total = total + other[block, g * height : (g + 1) * height]
            outs[far * groups + g][...] = total


def join(owner_slot, place, last, early, came, blocks, cores):
    positions, height, width = early[0].shape
    groups = len(early)
    return pl.pallas_call(
        functools.partial(join_kernel, positions + 1, cores, groups, blocks),
        out_shape=(jax.ShapeDtypeStruct((height, width), F32),) * (blocks * groups),
        in_specs=[SMEM, SMEM] + [VMEM] * (1 + groups + len(came)),
        out_specs=(VMEM,) * (blocks * groups),
        compiler_params=pltpu.CompilerParams(vmem_limit_bytes=VMEM_LIMIT),
    )(owner_slot, place, last, *early, *came)


def square_kernel(dp, terms, counts, wanted, place, act, *refs):
    parts, outs = refs[:terms], refs[terms:]
    row = place[0]
    total = parts[0][...]
    for part in parts[1:]:
        total = total + part[...]
    sequences = total.shape[0] // LEN
    rotated = []
    for s in range(sequences):
        position = lax.broadcasted_iota(jnp.int32, (LEN, total.shape[1]), 0)
        used = jnp.where(position < counts[s], total[s * LEN : (s + 1) * LEN], 0.0)
        rotated.append(used.astype(BF16))
    height = outs[0].shape[0]
    for step in range(dp):
        start = lax.rem(row + step, dp) * height
        first = wanted[0, start // BW] * BW + lax.rem(start, BW)
        rows = pl.ds(pl.multiple_of(first, height), height)
        square = None
        for s in range(sequences):
            product = jnp.dot(
                act[rows, s * LEN : (s + 1) * LEN], rotated[s], preferred_element_type=F32
            )
            square = product * product if square is None else square + product * product
        outs[step][...] = square.astype(outs[step].dtype)


def squares(counts, wanted, place, act, parts, height, dp):
    width = parts[0].shape[1]
    return pl.pallas_call(
        functools.partial(square_kernel, dp, len(parts)),
        out_shape=tuple(
            jax.ShapeDtypeStruct((height, width), F32 if step == 0 else BF16)
            for step in range(dp)
        ),
        in_specs=[SMEM, SMEM, SMEM, VMEM] + [VMEM] * len(parts),
        out_specs=(VMEM,) * dp,
        compiler_params=pltpu.CompilerParams(vmem_limit_bytes=VMEM_LIMIT),
    )(counts, wanted, place, act, *parts)


def on_device(
    activations, gradients, token_counts, basis_act, basis_store, owner_slot, reader_blocks
):
    seq_local = activations.shape[0]
    slots = seq_local * LEN
    groups, dp = lax.axis_size("groups"), lax.axis_size("dp")
    cores, blocks = lax.axis_size("cores"), lax.axis_size("block")
    group, row = lax.axis_index("groups"), lax.axis_index("dp")
    block, core = lax.axis_index("block"), lax.axis_index("cores")
    _, features, width = basis_store.shape
    part_features = features // groups
    place = jnp.stack([row, core, block])

    ring = [
        lax.dynamic_slice_in_dim(basis_store[0], group * part_features, part_features, 0)
    ]
    flat_grads = after(gradients.reshape(slots, features), ring[0])

    def share(index):
        return lax.dynamic_slice_in_dim(flat_grads, index * part_features, part_features, 1)

    away = [share((group + step) % groups) for step in range(1, groups)]
    others = [[shift(rows, "groups", step)] for step, rows in enumerate(away, 1)]

    flat_acts = activations.reshape(slots, activations.shape[2])
    act, *away_act = rotate(place, flat_acts, basis_act, blocks, cores)
    act_rot_t = None
    for step in range(1, dp):
        came = shift(ring[-1], "dp", 1)
        if step == 1:
            came, act, flat_grads, *away_act = lax.optimization_barrier(
                (came, act, flat_grads, *away_act)
            )
            for i, part in enumerate(away_act, 1):
                act = act + to_neighbour(part, i // cores, i % cores)
            rows = [[share(group)]] + others
        if step == 2:
            came, act = lax.optimization_barrier((came, act))
            act_rot_t = gather_act(act.astype(BF16))
        ring.append(came)

    early = [early_products(part, ring[:-1], (0,)) for part in rows]
    last, act_rot_t, *early = lax.optimization_barrier((ring[-1], act_rot_t, *early))
    last, *sends = pack(owner_slot, place, rows, last, early, blocks, cores)
    came = [shift(send, "cores", step) for step, send in enumerate(sends, 1)]
    parts = join(owner_slot, place, last, early, came, blocks, cores)

    parts = list(parts)
    for far in range(blocks):
        for back in range(groups):
            if far or back:
                pairs = [
                    (g * blocks + b, ((g - back) % groups) * blocks + (b + far) % blocks)
                    for g in range(groups)
                    for b in range(blocks)
                ]
                i = far * groups + back
                parts[i] = lax.ppermute(parts[i], ("groups", "block"), pairs)

    height = reader_blocks.shape[1] * BW // dp
    own, *others = squares(
        token_counts, reader_blocks, place, act_rot_t, parts, height, dp
    )
    for step in range(1, dp):
        own = own + shift(others[step - 1], "dp", step).astype(F32)
    return own / (seq_local * dp)


def solution(mesh):
    in_specs = (
        P(("groups", "dp"), None, ("block", "cores")),
        P(("groups", "dp"), None, ("block", "cores")),
        P(("groups", "dp")),
        P(("block", "cores"), None),
        P("dp", ("block", "cores"), None),
        P(),
        P(("block", "cores"), None),
    )
    out_specs = P(("groups", "dp"), ("block", "cores"))
    return jax.shard_map(
        on_device, mesh=mesh, in_specs=in_specs, out_specs=out_specs, check_vma=False
    )
```

```python
import functools

import jax
import jax.numpy as jnp
from jax import lax
from jax.experimental import pallas as pl
from jax.experimental.pallas import tpu as pltpu
from jax.sharding import PartitionSpec as P

BW = 512
LEN = 128
F32 = jnp.float32
BF16 = jnp.bfloat16
VMEM_LIMIT = 40 * 1024 * 1024
VMEM = pl.BlockSpec(memory_space=pltpu.VMEM)
SMEM = pl.BlockSpec(memory_space=pltpu.SMEM)


def after(value, *gates):
    return lax.optimization_barrier((value,) + gates)[0]


def shift(value, axis, step):
    size = lax.axis_size(axis)
    return lax.ppermute(value, axis, [(i, (i + step) % size) for i in range(size)])


def block_of(value, index):
    return lax.dynamic_index_in_dim(value, index, 0, keepdims=False)


def to_neighbour(value, far, step):
    cores, blocks = lax.axis_size("cores"), lax.axis_size("block")
    pairs = [
        (b * cores + c, (b + far) % blocks * cores + (c + step) % cores)
        for b in range(blocks)
        for c in range(cores)
    ]
    return lax.ppermute(value, ("block", "cores"), pairs)


def assemble_kernel(blocks, cores, place, *refs):
    parts, out = refs[:-1], refs[-1]
    height = parts[0].shape[0]
    for i, part in enumerate(parts):
        core = lax.rem(place[1] - i % cores + cores, cores)
        block = lax.rem(place[2] - i // cores + blocks, blocks)
        start = pl.multiple_of((core * blocks + block) * height, height)
        out[pl.ds(start, height)] = part[...]


def gather_act(place, act):
    cores, blocks = lax.axis_size("cores"), lax.axis_size("block")
    parts = [act] + [to_neighbour(act, i // cores, i % cores) for i in range(1, blocks * cores)]
    shape = (len(parts) * act.shape[0], act.shape[1])
    return pl.pallas_call(
        functools.partial(assemble_kernel, blocks, cores),
        out_shape=jax.ShapeDtypeStruct(shape, act.dtype),
        in_specs=[SMEM] + [VMEM] * len(parts),
        out_specs=VMEM,
        compiler_params=pltpu.CompilerParams(vmem_limit_bytes=VMEM_LIMIT),
    )(place, *parts)


def rotate_kernel(blocks, cores, place, acts, basis, *outs):
    height = outs[0].shape[0]
    for core_step in range(cores):
        core = lax.rem(place[1] + core_step, cores)
        span = blocks * height
        columns = pl.ds(pl.multiple_of(core * span, span), span)
        term = jnp.dot(acts[...], basis[:, columns], preferred_element_type=F32)
        for share in range(blocks):
            step = lax.rem(share - place[2] + blocks, blocks)
            part = term[:, share * height : (share + 1) * height].T
            for i in range(blocks):

                @pl.when(step == i)
                def _():
                    outs[i * cores + core_step][...] = part


def rotate(place, acts, basis, blocks, cores):
    shape = (basis.shape[1] // (blocks * cores), acts.shape[0])
    return pl.pallas_call(
        functools.partial(rotate_kernel, blocks, cores),
        out_shape=(jax.ShapeDtypeStruct(shape, F32),) * (blocks * cores),
        in_specs=[SMEM, VMEM, VMEM],
        out_specs=(VMEM,) * (blocks * cores),
        compiler_params=pltpu.CompilerParams(vmem_limit_bytes=VMEM_LIMIT),
    )(place, acts, basis)


def product(rows, piece, start):
    total, first = None, 0
    for part in rows:
        last = first + part.shape[1]
        low, high = max(first, start), min(last, start + piece.shape[0])
        if low < high:
            term = jnp.dot(
                part[:, low - first : high - first],
                piece[low - start : high - start],
                preferred_element_type=F32,
            )
            total = term if total is None else total + term
        first = last
    return total


def early_kernel(parts, shares, *refs):
    rows, pieces, out = refs[:parts], refs[parts:-1], refs[-1]
    for position in range(out.shape[0]):
        total = None
        for share, start in enumerate(shares):
            i = position * len(shares) + share
            if i < len(pieces):
                term = product(rows, pieces[i], start)
                total = term if total is None else total + term
        out[position] = total


def early_products(rows, pieces, shares):
    positions = -(-len(pieces) // len(shares))
    height, width = rows[0].shape[0], pieces[0].shape[1]
    flops = 2 * height * width * sum(piece.shape[0] for piece in pieces)
    return pl.pallas_call(
        functools.partial(early_kernel, len(rows), shares),
        out_shape=jax.ShapeDtypeStruct((positions, height, width), F32),
        in_specs=[VMEM] * (len(rows) + len(pieces)),
        out_specs=VMEM,
        compiler_params=pltpu.CompilerParams(vmem_limit_bytes=VMEM_LIMIT),
        cost_estimate=pl.CostEstimate(
            flops=flops, bytes_accessed=flops // width, transcendentals=0
        ),
    )(*rows, *pieces)


def total_of(position, early, last, group):
    positions = early[0].shape[0]
    height = early[0].shape[1]
    at_last = last[pl.ds(group * height, height)]
    before = early[group][jnp.minimum(position, positions - 1)]
    return jnp.where(position == positions, at_last, before)


def pack_kernel(dp, cores, parts, start, owner, place, held, *refs):
    row, core = place[0], place[1]
    refs = list(refs)
    rows = [[refs.pop(0) for _ in range(cuts)] for cuts in parts]
    early = [refs.pop(0) for _ in parts]
    almost = [refs.pop(0) for _ in parts]
    last, sends = refs[0], refs[1:]
    height = early[0].shape[1]
    for g in range(len(parts)):
        last[g * height : (g + 1) * height] = almost[g][0] + product(rows[g], held, start)
    for step in range(1, cores):
        for block in range(sends[0].shape[0]):
            piece = block * cores + lax.rem(core + step, cores)
            position = lax.rem(row - owner[piece] + dp, dp)
            for g in range(len(parts)):
                sends[step - 1][block, g * height : (g + 1) * height] = total_of(
                    position, early, last, g
                )


def pack(owner_slot, place, rows, held, start, early, almost, blocks, cores):
    positions, height, width = early[0].shape
    shape = (len(rows) * height, width)
    parts = tuple(len(part) for part in rows)
    return pl.pallas_call(
        functools.partial(pack_kernel, positions + 1, cores, parts, start),
        out_shape=(jax.ShapeDtypeStruct(shape, F32),)
        + (jax.ShapeDtypeStruct((blocks,) + shape, F32),) * (cores - 1),
        in_specs=[SMEM, SMEM] + [VMEM] * (1 + sum(parts) + 2 * len(rows)),
        out_specs=(VMEM,) * cores,
        compiler_params=pltpu.CompilerParams(vmem_limit_bytes=VMEM_LIMIT),
    )(owner_slot, place, held, *[cut for part in rows for cut in part], *early, *almost)


def join_kernel(dp, cores, groups, blocks, owner, place, last, *refs):
    row, core, me = place[0], place[1], place[2]
    early, came, outs = refs[:groups], refs[groups : groups + cores - 1], refs[groups + cores - 1 :]
    height = early[0].shape[1]
    for far in range(blocks):
        block = lax.rem(me + far, blocks)
        position = lax.rem(row - owner[block * cores + core] + dp, dp)
        for g in range(groups):
            total = total_of(position, early, last, g)
            for other in came:
                total = total + other[block, g * height : (g + 1) * height]
            outs[far * groups + g][...] = total


def join(owner_slot, place, last, early, came, blocks, cores):
    positions, height, width = early[0].shape
    groups = len(early)
    return pl.pallas_call(
        functools.partial(join_kernel, positions + 1, cores, groups, blocks),
        out_shape=(jax.ShapeDtypeStruct((height, width), F32),) * (blocks * groups),
        in_specs=[SMEM, SMEM] + [VMEM] * (1 + groups + len(came)),
        out_specs=(VMEM,) * (blocks * groups),
        compiler_params=pltpu.CompilerParams(vmem_limit_bytes=VMEM_LIMIT),
    )(owner_slot, place, last, *early, *came)


def square_kernel(dp, terms, counts, wanted, place, act, *refs):
    parts, outs = refs[:terms], refs[terms:]
    row = place[0]
    total = parts[0][...]
    for part in parts[1:]:
        total = total + part[...]
    sequences = total.shape[0] // LEN
    rotated = []
    for s in range(sequences):
        position = lax.broadcasted_iota(jnp.int32, (LEN, total.shape[1]), 0)
        used = jnp.where(position < counts[s], total[s * LEN : (s + 1) * LEN], 0.0)
        rotated.append(used.astype(BF16))
    height = outs[0].shape[0]
    for step in range(dp):
        start = lax.rem(row + step, dp) * height
        first = wanted[0, start // BW] * BW + lax.rem(start, BW)
        rows = pl.ds(pl.multiple_of(first, height), height)
        square = None
        for s in range(sequences):
            product = jnp.dot(
                act[rows, s * LEN : (s + 1) * LEN], rotated[s], preferred_element_type=F32
            )
            square = product * product if square is None else square + product * product
        outs[step][...] = square.astype(outs[step].dtype)


def squares(counts, wanted, place, act, parts, height, dp):
    width = parts[0].shape[1]
    return pl.pallas_call(
        functools.partial(square_kernel, dp, len(parts)),
        out_shape=tuple(
            jax.ShapeDtypeStruct((height, width), F32 if step == 0 else BF16)
            for step in range(dp)
        ),
        in_specs=[SMEM, SMEM, SMEM, VMEM] + [VMEM] * len(parts),
        out_specs=(VMEM,) * dp,
        compiler_params=pltpu.CompilerParams(vmem_limit_bytes=VMEM_LIMIT),
    )(counts, wanted, place, act, *parts)


def on_device(
    activations, gradients, token_counts, basis_act, basis_store, owner_slot, reader_blocks
):
    seq_local = activations.shape[0]
    slots = seq_local * LEN
    groups, dp = lax.axis_size("groups"), lax.axis_size("dp")
    cores, blocks = lax.axis_size("cores"), lax.axis_size("block")
    group, row = lax.axis_index("groups"), lax.axis_index("dp")
    block, core = lax.axis_index("block"), lax.axis_index("cores")
    _, features, width = basis_store.shape
    part_features = features // groups
    place = jnp.stack([row, core, block])

    cut = part_features // 256 * 128
    shares = (0, cut)
    first, second = [
        [lax.dynamic_slice_in_dim(basis_store[0], group * part_features + start, size, 0)]
        for start, size in zip(shares, (cut, part_features - cut))
    ]
    flat_grads = after(gradients.reshape(slots, features), first[0], second[0])

    def share(index):
        return lax.dynamic_slice_in_dim(flat_grads, index * part_features, part_features, 1)

    away = [share((group + step) % groups) for step in range(1, groups)]
    others = [[shift(rows, "groups", step)] for step, rows in enumerate(away, 1)]

    flat_acts = activations.reshape(slots, activations.shape[2])
    act, *away_act = rotate(place, flat_acts, basis_act, blocks, cores)
    for step in range(1, dp):
        first.append(shift(first[-1], "dp", 1))
        second.append(shift(second[-1], "dp", 1))
        if step == 1:
            first[1], act, flat_grads, *away_act = lax.optimization_barrier(
                (first[1], act, flat_grads, *away_act)
            )
            away_act = [
                to_neighbour(part, i // cores, i % cores) for i, part in enumerate(away_act, 1)
            ]
            rows = [[share(group)]] + others
    act = after(act, second[2])
    for part in away_act:
        act = act + part
    act_rot_t = gather_act(place, act.astype(BF16))

    pieces = [piece for pair in zip(first, second) for piece in pair]
    early = [early_products(part, pieces[:-2], shares) for part in rows]
    pieces[-2], *early = lax.optimization_barrier((pieces[-2], *early))
    almost = [early_products(part, pieces[-2:-1], shares[:1]) for part in rows]
    last, *almost = lax.optimization_barrier((pieces[-1], *almost))
    last, *sends = pack(owner_slot, place, rows, last, cut, early, almost, blocks, cores)
    came = [shift(send, "cores", step) for step, send in enumerate(sends, 1)]
    came[0], act_rot_t = lax.optimization_barrier((came[0], act_rot_t))
    parts = join(owner_slot, place, last, early, came, blocks, cores)

    parts = list(parts)
    for far in range(blocks):
        for back in range(groups):
            if far or back:
                pairs = [
                    (g * blocks + b, ((g - back) % groups) * blocks + (b + far) % blocks)
                    for g in range(groups)
                    for b in range(blocks)
                ]
                i = far * groups + back
                parts[i] = lax.ppermute(parts[i], ("groups", "block"), pairs)

    height = reader_blocks.shape[1] * BW // dp
    own, *others = squares(
        token_counts, reader_blocks, place, act_rot_t, parts, height, dp
    )
    for step in range(1, dp):
        own = own + shift(others[step - 1], "dp", step).astype(F32)
    return own / (seq_local * dp)


def solution(mesh):
    in_specs = (
        P(("groups", "dp"), None, ("block", "cores")),
        P(("groups", "dp"), None, ("block", "cores")),
        P(("groups", "dp")),
        P(("block", "cores"), None),
        P("dp", ("block", "cores"), None),
        P(),
        P(("block", "cores"), None),
    )
    out_specs = P(("groups", "dp"), ("block", "cores"))
    return jax.shard_map(
        on_device, mesh=mesh, in_specs=in_specs, out_specs=out_specs, check_vma=False
    )
```

```python
import functools

import jax
import jax.numpy as jnp
from jax import lax
from jax.experimental import pallas as pl
from jax.experimental.pallas import tpu as pltpu
from jax.sharding import PartitionSpec as P

BW = 512
LEN = 128
F32 = jnp.float32
BF16 = jnp.bfloat16
VMEM_LIMIT = 40 * 1024 * 1024
VMEM = pl.BlockSpec(memory_space=pltpu.VMEM)
SMEM = pl.BlockSpec(memory_space=pltpu.SMEM)


def after(value, *gates):
    return lax.optimization_barrier((value,) + gates)[0]


def shift(value, axis, step):
    size = lax.axis_size(axis)
    return lax.ppermute(value, axis, [(i, (i + step) % size) for i in range(size)])


def block_of(value, index):
    return lax.dynamic_index_in_dim(value, index, 0, keepdims=False)


def to_neighbour(value, far, step):
    cores, blocks = lax.axis_size("cores"), lax.axis_size("block")
    pairs = [
        (b * cores + c, (b + far) % blocks * cores + (c + step) % cores)
        for b in range(blocks)
        for c in range(cores)
    ]
    return lax.ppermute(value, ("block", "cores"), pairs)


def assemble_kernel(blocks, cores, place, *refs):
    parts, out = refs[:-1], refs[-1]
    height = parts[0].shape[0]
    for i, part in enumerate(parts):
        core = lax.rem(place[1] - i % cores + cores, cores)
        block = lax.rem(place[2] - i // cores + blocks, blocks)
        start = pl.multiple_of((core * blocks + block) * height, height)
        out[pl.ds(start, height)] = part[...]


def gather_act(place, act):
    cores, blocks = lax.axis_size("cores"), lax.axis_size("block")
    parts = [act] + [to_neighbour(act, i // cores, i % cores) for i in range(1, blocks * cores)]
    shape = (len(parts) * act.shape[0], act.shape[1])
    return pl.pallas_call(
        functools.partial(assemble_kernel, blocks, cores),
        out_shape=jax.ShapeDtypeStruct(shape, act.dtype),
        in_specs=[SMEM] + [VMEM] * len(parts),
        out_specs=VMEM,
        compiler_params=pltpu.CompilerParams(vmem_limit_bytes=VMEM_LIMIT),
    )(place, *parts)


def rotate_kernel(blocks, cores, place, acts, basis, *outs):
    height = outs[0].shape[0]
    for core_step in range(cores):
        core = lax.rem(place[1] + core_step, cores)
        span = blocks * height
        columns = pl.ds(pl.multiple_of(core * span, span), span)
        term = jnp.dot(acts[...], basis[:, columns], preferred_element_type=F32)
        for share in range(blocks):
            step = lax.rem(share - place[2] + blocks, blocks)
            part = term[:, share * height : (share + 1) * height].T
            for i in range(blocks):

                @pl.when(step == i)
                def _():
                    outs[i * cores + core_step][...] = part


def rotate(place, acts, basis, blocks, cores):
    shape = (basis.shape[1] // (blocks * cores), acts.shape[0])
    return pl.pallas_call(
        functools.partial(rotate_kernel, blocks, cores),
        out_shape=(jax.ShapeDtypeStruct(shape, F32),) * (blocks * cores),
        in_specs=[SMEM, VMEM, VMEM],
        out_specs=(VMEM,) * (blocks * cores),
        compiler_params=pltpu.CompilerParams(vmem_limit_bytes=VMEM_LIMIT),
    )(place, acts, basis)


def product(rows, piece, start):
    total, first = None, 0
    for part in rows:
        last = first + part.shape[1]
        low, high = max(first, start), min(last, start + piece.shape[0])
        if low < high:
            term = jnp.dot(
                part[:, low - first : high - first],
                piece[low - start : high - start],
                preferred_element_type=F32,
            )
            total = term if total is None else total + term
        first = last
    return total


def early_kernel(parts, shares, *refs):
    rows, pieces, out = refs[:parts], refs[parts:-1], refs[-1]
    for position in range(out.shape[0]):
        total = None
        for share, start in enumerate(shares):
            i = position * len(shares) + share
            if i < len(pieces):
                term = product(rows, pieces[i], start)
                total = term if total is None else total + term
        out[position] = total


def early_products(rows, pieces, shares):
    positions = -(-len(pieces) // len(shares))
    height, width = rows[0].shape[0], pieces[0].shape[1]
    flops = 2 * height * width * sum(piece.shape[0] for piece in pieces)
    return pl.pallas_call(
        functools.partial(early_kernel, len(rows), shares),
        out_shape=jax.ShapeDtypeStruct((positions, height, width), F32),
        in_specs=[VMEM] * (len(rows) + len(pieces)),
        out_specs=VMEM,
        compiler_params=pltpu.CompilerParams(vmem_limit_bytes=VMEM_LIMIT),
        cost_estimate=pl.CostEstimate(
            flops=flops, bytes_accessed=flops // width, transcendentals=0
        ),
    )(*rows, *pieces)


def total_of(position, early, last, group):
    positions = early[0].shape[0]
    height = early[0].shape[1]
    at_last = last[pl.ds(group * height, height)]
    before = early[group][jnp.minimum(position, positions - 1)]
    return jnp.where(position == positions, at_last, before)


def pack_kernel(dp, cores, parts, start, owner, place, held, *refs):
    row, core = place[0], place[1]
    refs = list(refs)
    rows = [[refs.pop(0) for _ in range(cuts)] for cuts in parts]
    early = [refs.pop(0) for _ in parts]
    almost = [refs.pop(0) for _ in parts]
    last, sends = refs[0], refs[1:]
    height = early[0].shape[1]
    for g in range(len(parts)):
        last[g * height : (g + 1) * height] = almost[g][0] + product(rows[g], held, start)
    for step in range(1, cores):
        for block in range(sends[0].shape[0]):
            piece = block * cores + lax.rem(core + step, cores)
            position = lax.rem(row - owner[piece] + dp, dp)
            for g in range(len(parts)):
                sends[step - 1][block, g * height : (g + 1) * height] = total_of(
                    position, early, last, g
                )


def pack(owner_slot, place, rows, held, start, early, almost, blocks, cores):
    positions, height, width = early[0].shape
    shape = (len(rows) * height, width)
    parts = tuple(len(part) for part in rows)
    return pl.pallas_call(
        functools.partial(pack_kernel, positions + 1, cores, parts, start),
        out_shape=(jax.ShapeDtypeStruct(shape, F32),)
        + (jax.ShapeDtypeStruct((blocks,) + shape, F32),) * (cores - 1),
        in_specs=[SMEM, SMEM] + [VMEM] * (1 + sum(parts) + 2 * len(rows)),
        out_specs=(VMEM,) * cores,
        compiler_params=pltpu.CompilerParams(vmem_limit_bytes=VMEM_LIMIT),
    )(owner_slot, place, held, *[cut for part in rows for cut in part], *early, *almost)


def join_kernel(dp, cores, groups, blocks, owner, place, last, *refs):
    row, core, me = place[0], place[1], place[2]
    early, came, outs = refs[:groups], refs[groups : groups + cores - 1], refs[groups + cores - 1 :]
    height = early[0].shape[1]
    for far in range(blocks):
        block = lax.rem(me + far, blocks)
        position = lax.rem(row - owner[block * cores + core] + dp, dp)
        for g in range(groups):
            total = total_of(position, early, last, g)
            for other in came:
                total = total + other[block, g * height : (g + 1) * height]
            outs[far * groups + g][...] = total


def join(owner_slot, place, last, early, came, blocks, cores):
    positions, height, width = early[0].shape
    groups = len(early)
    return pl.pallas_call(
        functools.partial(join_kernel, positions + 1, cores, groups, blocks),
        out_shape=(jax.ShapeDtypeStruct((height, width), F32),) * (blocks * groups),
        in_specs=[SMEM, SMEM] + [VMEM] * (1 + groups + len(came)),
        out_specs=(VMEM,) * (blocks * groups),
        compiler_params=pltpu.CompilerParams(vmem_limit_bytes=VMEM_LIMIT),
    )(owner_slot, place, last, *early, *came)


def square_kernel(dp, terms, counts, wanted, place, act, *refs):
    parts, outs = refs[:terms], refs[terms:]
    row = place[0]
    total = parts[0][...]
    for part in parts[1:]:
        total = total + part[...]
    sequences = total.shape[0] // LEN
    rotated = []
    for s in range(sequences):
        position = lax.broadcasted_iota(jnp.int32, (LEN, total.shape[1]), 0)
        used = jnp.where(position < counts[s], total[s * LEN : (s + 1) * LEN], 0.0)
        rotated.append(used.astype(BF16))
    height = outs[0].shape[0]
    for step in range(dp):
        start = lax.rem(row + step, dp) * height
        first = wanted[0, start // BW] * BW + lax.rem(start, BW)
        rows = pl.ds(pl.multiple_of(first, height), height)
        square = None
        for s in range(sequences):
            product = jnp.dot(
                act[rows, s * LEN : (s + 1) * LEN], rotated[s], preferred_element_type=F32
            )
            square = product * product if square is None else square + product * product
        outs[step][...] = square.astype(outs[step].dtype)


def squares(counts, wanted, place, act, parts, height, dp):
    width = parts[0].shape[1]
    return pl.pallas_call(
        functools.partial(square_kernel, dp, len(parts)),
        out_shape=tuple(
            jax.ShapeDtypeStruct((height, width), F32 if step == 0 else BF16)
            for step in range(dp)
        ),
        in_specs=[SMEM, SMEM, SMEM, VMEM] + [VMEM] * len(parts),
        out_specs=(VMEM,) * dp,
        compiler_params=pltpu.CompilerParams(vmem_limit_bytes=VMEM_LIMIT),
    )(counts, wanted, place, act, *parts)


def on_device(
    activations, gradients, token_counts, basis_act, basis_store, owner_slot, reader_blocks
):
    seq_local = activations.shape[0]
    slots = seq_local * LEN
    groups, dp = lax.axis_size("groups"), lax.axis_size("dp")
    cores, blocks = lax.axis_size("cores"), lax.axis_size("block")
    group, row = lax.axis_index("groups"), lax.axis_index("dp")
    block, core = lax.axis_index("block"), lax.axis_index("cores")
    _, features, width = basis_store.shape
    part_features = features // groups
    place = jnp.stack([row, core, block])

    cut = part_features // 256 * 128
    shares = (0, cut)
    first, second = [
        [lax.dynamic_slice_in_dim(basis_store[0], group * part_features + start, size, 0)]
        for start, size in zip(shares, (cut, part_features - cut))
    ]
    flat_grads = after(gradients.reshape(slots, features), first[0], second[0])

    def share(index):
        return lax.dynamic_slice_in_dim(flat_grads, index * part_features, part_features, 1)

    away = [share((group + step) % groups) for step in range(1, groups)]
    others = [[shift(rows, "groups", step)] for step, rows in enumerate(away, 1)]

    flat_acts = activations.reshape(slots, activations.shape[2])
    act, *away_act = rotate(place, flat_acts, basis_act, blocks, cores)
    for step in range(1, dp):
        first.append(shift(first[-1], "dp", 1))
        second.append(shift(second[-1], "dp", 1))
        if step == 1:
            first[1], act, flat_grads, *away_act = lax.optimization_barrier(
                (first[1], act, flat_grads, *away_act)
            )
            away_act = [
                to_neighbour(part, i // cores, i % cores) for i, part in enumerate(away_act, 1)
            ]
            rows = [[share(group)]] + others
    act = after(act, first[2], second[2])
    for part in away_act:
        act = act + part
    act_rot_t = gather_act(place, act.astype(BF16))

    pieces = [piece for pair in zip(first, second) for piece in pair]
    early = [early_products(part, pieces[:-2], shares) for part in rows]
    almost = [early_products(part, pieces[-2:-1], shares[:1]) for part in rows]
    last, act_rot_t, *done = lax.optimization_barrier((pieces[-1], act_rot_t, *almost, *early))
    almost, early = done[: len(rows)], done[len(rows) :]
    last, *sends = pack(owner_slot, place, rows, last, cut, early, almost, blocks, cores)
    came = [shift(send, "cores", step) for step, send in enumerate(sends, 1)]
    parts = join(owner_slot, place, last, early, came, blocks, cores)

    parts = list(parts)
    for far in range(blocks):
        for back in range(groups):
            if far or back:
                pairs = [
                    (g * blocks + b, ((g - back) % groups) * blocks + (b + far) % blocks)
                    for g in range(groups)
                    for b in range(blocks)
                ]
                i = far * groups + back
                parts[i] = lax.ppermute(parts[i], ("groups", "block"), pairs)

    height = reader_blocks.shape[1] * BW // dp
    own, *others = squares(
        token_counts, reader_blocks, place, act_rot_t, parts, height, dp
    )
    for step in range(1, dp):
        own = own + shift(others[step - 1], "dp", step).astype(F32)
    return own / (seq_local * dp)


def solution(mesh):
    in_specs = (
        P(("groups", "dp"), None, ("block", "cores")),
        P(("groups", "dp"), None, ("block", "cores")),
        P(("groups", "dp")),
        P(("block", "cores"), None),
        P("dp", ("block", "cores"), None),
        P(),
        P(("block", "cores"), None),
    )
    out_specs = P(("groups", "dp"), ("block", "cores"))
    return jax.shard_map(
        on_device, mesh=mesh, in_specs=in_specs, out_specs=out_specs, check_vma=False
    )
```

```python
import functools

import jax
import jax.numpy as jnp
from jax import lax
from jax.experimental import pallas as pl
from jax.experimental.pallas import tpu as pltpu
from jax.sharding import PartitionSpec as P

BW = 512
LEN = 128
F32 = jnp.float32
BF16 = jnp.bfloat16
VMEM_LIMIT = 40 * 1024 * 1024
VMEM = pl.BlockSpec(memory_space=pltpu.VMEM)
SMEM = pl.BlockSpec(memory_space=pltpu.SMEM)


def after(value, *gates):
    return lax.optimization_barrier((value,) + gates)[0]


def shift(value, axis, step):
    size = lax.axis_size(axis)
    return lax.ppermute(value, axis, [(i, (i + step) % size) for i in range(size)])


def block_of(value, index):
    return lax.dynamic_index_in_dim(value, index, 0, keepdims=False)


def to_neighbour(value, far, step):
    cores, blocks = lax.axis_size("cores"), lax.axis_size("block")
    pairs = [
        (b * cores + c, (b + far) % blocks * cores + (c + step) % cores)
        for b in range(blocks)
        for c in range(cores)
    ]
    return lax.ppermute(value, ("block", "cores"), pairs)


def assemble_kernel(blocks, cores, place, *refs):
    parts, out = refs[:-1], refs[-1]
    height = parts[0].shape[0]
    for i, part in enumerate(parts):
        core = lax.rem(place[1] - i % cores + cores, cores)
        block = lax.rem(place[2] - i // cores + blocks, blocks)
        start = pl.multiple_of((core * blocks + block) * height, height)
        out[pl.ds(start, height)] = part[...]


def gather_act(act, gate):
    cores, blocks = lax.axis_size("cores"), lax.axis_size("block")
    sent = [after(act, gate) if i == 1 else act for i in range(blocks * cores)]
    parts = [act] + [to_neighbour(sent[i], i // cores, i % cores) for i in range(1, len(sent))]
    return parts


def assemble(place, parts, blocks, cores):
    shape = (len(parts) * parts[0].shape[0], parts[0].shape[1])
    return pl.pallas_call(
        functools.partial(assemble_kernel, blocks, cores),
        out_shape=jax.ShapeDtypeStruct(shape, BF16),
        in_specs=[SMEM] + [VMEM] * len(parts),
        out_specs=VMEM,
        compiler_params=pltpu.CompilerParams(vmem_limit_bytes=VMEM_LIMIT),
    )(place, *parts)


def rotate_kernel(blocks, cores, place, acts, basis, *outs):
    height = outs[0].shape[0]
    for core_step in range(cores):
        core = lax.rem(place[1] + core_step, cores)
        span = blocks * height
        columns = pl.ds(pl.multiple_of(core * span, span), span)
        term = jnp.dot(acts[...], basis[:, columns], preferred_element_type=F32)
        for share in range(blocks):
            step = lax.rem(share - place[2] + blocks, blocks)
            part = term[:, share * height : (share + 1) * height].T
            for i in range(blocks):

                @pl.when(step == i)
                def _():
                    outs[i * cores + core_step][...] = part


def rotate(place, acts, basis, blocks, cores):
    shape = (basis.shape[1] // (blocks * cores), acts.shape[0])
    return pl.pallas_call(
        functools.partial(rotate_kernel, blocks, cores),
        out_shape=(jax.ShapeDtypeStruct(shape, F32),) * (blocks * cores),
        in_specs=[SMEM, VMEM, VMEM],
        out_specs=(VMEM,) * (blocks * cores),
        compiler_params=pltpu.CompilerParams(vmem_limit_bytes=VMEM_LIMIT),
    )(place, acts, basis)


def product(rows, piece, start):
    total, first = None, 0
    for part in rows:
        last = first + part.shape[1]
        low, high = max(first, start), min(last, start + piece.shape[0])
        if low < high:
            term = jnp.dot(
                part[:, low - first : high - first],
                piece[low - start : high - start],
                preferred_element_type=F32,
            )
            total = term if total is None else total + term
        first = last
    return total


def early_kernel(parts, shares, *refs):
    rows, pieces, out = refs[:parts], refs[parts:-1], refs[-1]
    for position in range(out.shape[0]):
        total = None
        for share, start in enumerate(shares):
            i = position * len(shares) + share
            if i < len(pieces):
                term = product(rows, pieces[i], start)
                total = term if total is None else total + term
        out[position] = total


def early_products(rows, pieces, shares):
    positions = -(-len(pieces) // len(shares))
    height, width = rows[0].shape[0], pieces[0].shape[1]
    flops = 2 * height * width * sum(piece.shape[0] for piece in pieces)
    return pl.pallas_call(
        functools.partial(early_kernel, len(rows), shares),
        out_shape=jax.ShapeDtypeStruct((positions, height, width), F32),
        in_specs=[VMEM] * (len(rows) + len(pieces)),
        out_specs=VMEM,
        compiler_params=pltpu.CompilerParams(vmem_limit_bytes=VMEM_LIMIT),
        cost_estimate=pl.CostEstimate(
            flops=flops, bytes_accessed=flops // width, transcendentals=0
        ),
    )(*rows, *pieces)


def total_of(position, early, last, group):
    positions = early[0].shape[0]
    height = early[0].shape[1]
    at_last = last[pl.ds(group * height, height)]
    before = early[group][jnp.minimum(position, positions - 1)]
    return jnp.where(position == positions, at_last, before)


def pack_kernel(dp, cores, parts, start, owner, place, held, *refs):
    row, core = place[0], place[1]
    refs = list(refs)
    rows = [[refs.pop(0) for _ in range(cuts)] for cuts in parts]
    early = [refs.pop(0) for _ in parts]
    almost = [refs.pop(0) for _ in parts]
    last, sends = refs[0], refs[1:]
    height = early[0].shape[1]
    for g in range(len(parts)):
        last[g * height : (g + 1) * height] = almost[g][0] + product(rows[g], held, start)
    for step in range(1, cores):
        for block in range(sends[0].shape[0]):
            piece = block * cores + lax.rem(core + step, cores)
            position = lax.rem(row - owner[piece] + dp, dp)
            for g in range(len(parts)):
                sends[step - 1][block, g * height : (g + 1) * height] = total_of(
                    position, early, last, g
                )


def pack(owner_slot, place, rows, held, start, early, almost, blocks, cores):
    positions, height, width = early[0].shape
    shape = (len(rows) * height, width)
    parts = tuple(len(part) for part in rows)
    return pl.pallas_call(
        functools.partial(pack_kernel, positions + 1, cores, parts, start),
        out_shape=(jax.ShapeDtypeStruct(shape, F32),)
        + (jax.ShapeDtypeStruct((blocks,) + shape, F32),) * (cores - 1),
        in_specs=[SMEM, SMEM] + [VMEM] * (1 + sum(parts) + 2 * len(rows)),
        out_specs=(VMEM,) * cores,
        compiler_params=pltpu.CompilerParams(vmem_limit_bytes=VMEM_LIMIT),
    )(owner_slot, place, held, *[cut for part in rows for cut in part], *early, *almost)


def join_kernel(dp, cores, groups, blocks, owner, place, last, *refs):
    row, core, me = place[0], place[1], place[2]
    early, came, outs = refs[:groups], refs[groups : groups + cores - 1], refs[groups + cores - 1 :]
    height = early[0].shape[1]
    for far in range(blocks):
        block = lax.rem(me + far, blocks)
        position = lax.rem(row - owner[block * cores + core] + dp, dp)
        for g in range(groups):
            total = total_of(position, early, last, g)
            for other in came:
                total = total + other[block, g * height : (g + 1) * height]
            outs[far * groups + g][...] = total


def join(owner_slot, place, last, early, came, blocks, cores):
    positions, height, width = early[0].shape
    groups = len(early)
    return pl.pallas_call(
        functools.partial(join_kernel, positions + 1, cores, groups, blocks),
        out_shape=(jax.ShapeDtypeStruct((height, width), F32),) * (blocks * groups),
        in_specs=[SMEM, SMEM] + [VMEM] * (1 + groups + len(came)),
        out_specs=(VMEM,) * (blocks * groups),
        compiler_params=pltpu.CompilerParams(vmem_limit_bytes=VMEM_LIMIT),
    )(owner_slot, place, last, *early, *came)


def square_kernel(dp, terms, counts, wanted, place, act, *refs):
    parts, outs = refs[:terms], refs[terms:]
    row = place[0]
    total = parts[0][...]
    for part in parts[1:]:
        total = total + part[...]
    sequences = total.shape[0] // LEN
    rotated = []
    for s in range(sequences):
        position = lax.broadcasted_iota(jnp.int32, (LEN, total.shape[1]), 0)
        used = jnp.where(position < counts[s], total[s * LEN : (s + 1) * LEN], 0.0)
        rotated.append(used.astype(BF16))
    height = outs[0].shape[0]
    for step in range(dp):
        start = lax.rem(row + step, dp) * height
        first = wanted[0, start // BW] * BW + lax.rem(start, BW)
        rows = pl.ds(pl.multiple_of(first, height), height)
        square = None
        for s in range(sequences):
            product = jnp.dot(
                act[rows, s * LEN : (s + 1) * LEN], rotated[s], preferred_element_type=F32
            )
            square = product * product if square is None else square + product * product
        outs[step][...] = square.astype(outs[step].dtype)


def squares(counts, wanted, place, act, parts, height, dp):
    width = parts[0].shape[1]
    return pl.pallas_call(
        functools.partial(square_kernel, dp, len(parts)),
        out_shape=tuple(
            jax.ShapeDtypeStruct((height, width), F32 if step == 0 else BF16)
            for step in range(dp)
        ),
        in_specs=[SMEM, SMEM, SMEM, VMEM] + [VMEM] * len(parts),
        out_specs=(VMEM,) * dp,
        compiler_params=pltpu.CompilerParams(vmem_limit_bytes=VMEM_LIMIT),
    )(counts, wanted, place, act, *parts)


def on_device(
    activations, gradients, token_counts, basis_act, basis_store, owner_slot, reader_blocks
):
    seq_local = activations.shape[0]
    slots = seq_local * LEN
    groups, dp = lax.axis_size("groups"), lax.axis_size("dp")
    cores, blocks = lax.axis_size("cores"), lax.axis_size("block")
    group, row = lax.axis_index("groups"), lax.axis_index("dp")
    block, core = lax.axis_index("block"), lax.axis_index("cores")
    _, features, width = basis_store.shape
    part_features = features // groups
    place = jnp.stack([row, core, block])

    cut = part_features // 256 * 128
    shares = (0, cut)
    first, second = [
        [lax.dynamic_slice_in_dim(basis_store[0], group * part_features + start, size, 0)]
        for start, size in zip(shares, (cut, part_features - cut))
    ]
    flat_grads = after(gradients.reshape(slots, features), first[0], second[0])

    def share(index):
        return lax.dynamic_slice_in_dim(flat_grads, index * part_features, part_features, 1)

    away = [share((group + step) % groups) for step in range(1, groups)]
    others = [[shift(rows, "groups", step)] for step, rows in enumerate(away, 1)]

    flat_acts = activations.reshape(slots, activations.shape[2])
    act, *away_act = rotate(place, flat_acts, basis_act, blocks, cores)
    for step in range(1, dp):
        first.append(shift(first[-1], "dp", 1))
        second.append(shift(second[-1], "dp", 1))
        if step == 1:
            first[1], act, flat_grads, *away_act = lax.optimization_barrier(
                (first[1], act, flat_grads, *away_act)
            )
            away_act = [
                to_neighbour(part, i // cores, i % cores) for i, part in enumerate(away_act, 1)
            ]
            rows = [[share(group)]] + others
    act = after(act, first[2])
    for i, part in enumerate(away_act):
        act = act + (after(part, first[-1]) if i == 0 else part)
    act_parts = gather_act(act.astype(BF16), first[-1])

    pieces = [piece for pair in zip(first, second) for piece in pair]
    early = [early_products(part, pieces[:-2], shares) for part in rows]
    almost = [early_products(part, pieces[-2:-1], shares[:1]) for part in rows]
    act_rot_t = assemble(after(place, *early, *almost), act_parts, blocks, cores)
    last, act_rot_t, *done = lax.optimization_barrier((pieces[-1], act_rot_t, *almost, *early))
    almost, early = done[: len(rows)], done[len(rows) :]
    last, *sends = pack(owner_slot, place, rows, last, cut, early, almost, blocks, cores)
    came = [shift(send, "cores", step) for step, send in enumerate(sends, 1)]
    parts = join(owner_slot, place, last, early, came, blocks, cores)

    parts = list(parts)
    for far in range(blocks):
        for back in range(groups):
            if far or back:
                pairs = [
                    (g * blocks + b, ((g - back) % groups) * blocks + (b + far) % blocks)
                    for g in range(groups)
                    for b in range(blocks)
                ]
                i = far * groups + back
                parts[i] = lax.ppermute(parts[i], ("groups", "block"), pairs)

    height = reader_blocks.shape[1] * BW // dp
    own, *others = squares(
        token_counts, reader_blocks, place, act_rot_t, parts, height, dp
    )
    for step in range(1, dp):
        own = own + shift(others[step - 1], "dp", step).astype(F32)
    return own / (seq_local * dp)


def solution(mesh):
    in_specs = (
        P(("groups", "dp"), None, ("block", "cores")),
        P(("groups", "dp"), None, ("block", "cores")),
        P(("groups", "dp")),
        P(("block", "cores"), None),
        P("dp", ("block", "cores"), None),
        P(),
        P(("block", "cores"), None),
    )
    out_specs = P(("groups", "dp"), ("block", "cores"))
    return jax.shard_map(
        on_device, mesh=mesh, in_specs=in_specs, out_specs=out_specs, check_vma=False
    )
```

```python
import functools

import jax
import jax.numpy as jnp
from jax import lax
from jax.experimental import pallas as pl
from jax.experimental.pallas import tpu as pltpu
from jax.sharding import PartitionSpec as P

BW = 512
LEN = 128
F32 = jnp.float32
BF16 = jnp.bfloat16
VMEM_LIMIT = 40 * 1024 * 1024
VMEM = pl.BlockSpec(memory_space=pltpu.VMEM)
SMEM = pl.BlockSpec(memory_space=pltpu.SMEM)


def after(value, *gates):
    return lax.optimization_barrier((value,) + gates)[0]


def shift(value, axis, step):
    size = lax.axis_size(axis)
    return lax.ppermute(value, axis, [(i, (i + step) % size) for i in range(size)])


def block_of(value, index):
    return lax.dynamic_index_in_dim(value, index, 0, keepdims=False)


def to_neighbour(value, far, step):
    cores, blocks = lax.axis_size("cores"), lax.axis_size("block")
    pairs = [
        (b * cores + c, (b + far) % blocks * cores + (c + step) % cores)
        for b in range(blocks)
        for c in range(cores)
    ]
    return lax.ppermute(value, ("block", "cores"), pairs)


def assemble_kernel(blocks, cores, place, *refs):
    parts, out = refs[:-1], refs[-1]
    height = parts[0].shape[0]
    for i, part in enumerate(parts):
        core = lax.rem(place[1] - i % cores + cores, cores)
        block = lax.rem(place[2] - i // cores + blocks, blocks)
        start = pl.multiple_of((core * blocks + block) * height, height)
        out[pl.ds(start, height)] = part[...]


def gather_act(act, gate):
    cores, blocks = lax.axis_size("cores"), lax.axis_size("block")
    sent = [after(act, *gate) if i == 1 else act for i in range(blocks * cores)]
    parts = [act] + [to_neighbour(sent[i], i // cores, i % cores) for i in range(1, len(sent))]
    return parts


def assemble(place, parts, blocks, cores):
    shape = (len(parts) * parts[0].shape[0], parts[0].shape[1])
    return pl.pallas_call(
        functools.partial(assemble_kernel, blocks, cores),
        out_shape=jax.ShapeDtypeStruct(shape, BF16),
        in_specs=[SMEM] + [VMEM] * len(parts),
        out_specs=VMEM,
        compiler_params=pltpu.CompilerParams(vmem_limit_bytes=VMEM_LIMIT),
    )(place, *parts)


def rotate_kernel(blocks, cores, place, acts, basis, *outs):
    height = outs[0].shape[0]
    for core_step in range(cores):
        core = lax.rem(place[1] + core_step, cores)
        span = blocks * height
        columns = pl.ds(pl.multiple_of(core * span, span), span)
        term = jnp.dot(acts[...], basis[:, columns], preferred_element_type=F32)
        for share in range(blocks):
            step = lax.rem(share - place[2] + blocks, blocks)
            part = term[:, share * height : (share + 1) * height].T
            for i in range(blocks):

                @pl.when(step == i)
                def _():
                    outs[i * cores + core_step][...] = part


def rotate(place, acts, basis, blocks, cores):
    shape = (basis.shape[1] // (blocks * cores), acts.shape[0])
    return pl.pallas_call(
        functools.partial(rotate_kernel, blocks, cores),
        out_shape=(jax.ShapeDtypeStruct(shape, F32),) * (blocks * cores),
        in_specs=[SMEM, VMEM, VMEM],
        out_specs=(VMEM,) * (blocks * cores),
        compiler_params=pltpu.CompilerParams(vmem_limit_bytes=VMEM_LIMIT),
    )(place, acts, basis)


def product(rows, piece, start):
    total, first = None, 0
    for part in rows:
        last = first + part.shape[1]
        low, high = max(first, start), min(last, start + piece.shape[0])
        if low < high:
            term = jnp.dot(
                part[:, low - first : high - first],
                piece[low - start : high - start],
                preferred_element_type=F32,
            )
            total = term if total is None else total + term
        first = last
    return total


def early_kernel(parts, shares, *refs):
    rows, pieces, out = refs[:parts], refs[parts:-1], refs[-1]
    for position in range(out.shape[0]):
        total = None
        for share, start in enumerate(shares):
            i = position * len(shares) + share
            if i < len(pieces):
                term = product(rows, pieces[i], start)
                total = term if total is None else total + term
        out[position] = total


def early_products(rows, pieces, shares):
    positions = -(-len(pieces) // len(shares))
    height, width = rows[0].shape[0], pieces[0].shape[1]
    flops = 2 * height * width * sum(piece.shape[0] for piece in pieces)
    return pl.pallas_call(
        functools.partial(early_kernel, len(rows), shares),
        out_shape=jax.ShapeDtypeStruct((positions, height, width), F32),
        in_specs=[VMEM] * (len(rows) + len(pieces)),
        out_specs=VMEM,
        compiler_params=pltpu.CompilerParams(vmem_limit_bytes=VMEM_LIMIT),
        cost_estimate=pl.CostEstimate(
            flops=flops, bytes_accessed=flops // width, transcendentals=0
        ),
    )(*rows, *pieces)


def total_of(position, early, rest, last, group):
    positions = early[0].shape[0]
    height = early[0].shape[1]
    at_last = last[pl.ds(group * height, height)]
    before = early[group][jnp.minimum(position, positions - 1)]
    late = jnp.where(position == positions, rest[group][0], at_last)
    return jnp.where(position < positions, before, late)


def pack_kernel(dp, cores, parts, start, owner, place, held, *refs):
    row, core = place[0], place[1]
    refs = list(refs)
    rows = [[refs.pop(0) for _ in range(cuts)] for cuts in parts]
    early = [refs.pop(0) for _ in parts]
    rest = [refs.pop(0) for _ in parts]
    last, sends = refs[0], refs[1:]
    height = early[0].shape[1]
    for g in range(len(parts)):
        last[g * height : (g + 1) * height] = rest[g][1] + product(rows[g], held, start)
    for step in range(1, cores):
        for block in range(sends[0].shape[0]):
            piece = block * cores + lax.rem(core + step, cores)
            position = lax.rem(row - owner[piece] + dp, dp)
            for g in range(len(parts)):
                sends[step - 1][block, g * height : (g + 1) * height] = total_of(
                    position, early, rest, last, g
                )


def pack(owner_slot, place, rows, held, start, early, rest, blocks, cores):
    positions, height, width = early[0].shape
    shape = (len(rows) * height, width)
    parts = tuple(len(part) for part in rows)
    return pl.pallas_call(
        functools.partial(pack_kernel, positions + 2, cores, parts, start),
        out_shape=(jax.ShapeDtypeStruct(shape, F32),)
        + (jax.ShapeDtypeStruct((blocks,) + shape, F32),) * (cores - 1),
        in_specs=[SMEM, SMEM] + [VMEM] * (1 + sum(parts) + 2 * len(rows)),
        out_specs=(VMEM,) * cores,
        compiler_params=pltpu.CompilerParams(vmem_limit_bytes=VMEM_LIMIT),
    )(owner_slot, place, held, *[cut for part in rows for cut in part], *early, *rest)


def join_kernel(dp, cores, groups, blocks, owner, place, last, *refs):
    row, core, me = place[0], place[1], place[2]
    early, rest, refs = refs[:groups], refs[groups : 2 * groups], refs[2 * groups :]
    came, outs = refs[: cores - 1], refs[cores - 1 :]
    height = early[0].shape[1]
    for far in range(blocks):
        block = lax.rem(me + far, blocks)
        position = lax.rem(row - owner[block * cores + core] + dp, dp)
        for g in range(groups):
            total = total_of(position, early, rest, last, g)
            for other in came:
                total = total + other[block, g * height : (g + 1) * height]
            outs[far * groups + g][...] = total


def join(owner_slot, place, last, early, rest, came, blocks, cores):
    positions, height, width = early[0].shape
    groups = len(early)
    return pl.pallas_call(
        functools.partial(join_kernel, positions + 2, cores, groups, blocks),
        out_shape=(jax.ShapeDtypeStruct((height, width), F32),) * (blocks * groups),
        in_specs=[SMEM, SMEM] + [VMEM] * (1 + 2 * groups + len(came)),
        out_specs=(VMEM,) * (blocks * groups),
        compiler_params=pltpu.CompilerParams(vmem_limit_bytes=VMEM_LIMIT),
    )(owner_slot, place, last, *early, *rest, *came)


def square_kernel(dp, terms, counts, wanted, place, act, *refs):
    parts, outs = refs[:terms], refs[terms:]
    row = place[0]
    total = parts[0][...]
    for part in parts[1:]:
        total = total + part[...]
    sequences = total.shape[0] // LEN
    rotated = []
    for s in range(sequences):
        position = lax.broadcasted_iota(jnp.int32, (LEN, total.shape[1]), 0)
        used = jnp.where(position < counts[s], total[s * LEN : (s + 1) * LEN], 0.0)
        rotated.append(used.astype(BF16))
    height = outs[0].shape[0]
    for step in range(dp):
        start = lax.rem(row + step, dp) * height
        first = wanted[0, start // BW] * BW + lax.rem(start, BW)
        rows = pl.ds(pl.multiple_of(first, height), height)
        square = None
        for s in range(sequences):
            product = jnp.dot(
                act[rows, s * LEN : (s + 1) * LEN], rotated[s], preferred_element_type=F32
            )
            square = product * product if square is None else square + product * product
        outs[step][...] = square.astype(outs[step].dtype)


def squares(counts, wanted, place, act, parts, height, dp):
    width = parts[0].shape[1]
    return pl.pallas_call(
        functools.partial(square_kernel, dp, len(parts)),
        out_shape=tuple(
            jax.ShapeDtypeStruct((height, width), F32 if step == 0 else BF16)
            for step in range(dp)
        ),
        in_specs=[SMEM, SMEM, SMEM, VMEM] + [VMEM] * len(parts),
        out_specs=(VMEM,) * dp,
        compiler_params=pltpu.CompilerParams(vmem_limit_bytes=VMEM_LIMIT),
    )(counts, wanted, place, act, *parts)


def on_device(
    activations, gradients, token_counts, basis_act, basis_store, owner_slot, reader_blocks
):
    seq_local = activations.shape[0]
    slots = seq_local * LEN
    groups, dp = lax.axis_size("groups"), lax.axis_size("dp")
    cores, blocks = lax.axis_size("cores"), lax.axis_size("block")
    group, row = lax.axis_index("groups"), lax.axis_index("dp")
    block, core = lax.axis_index("block"), lax.axis_index("cores")
    _, features, width = basis_store.shape
    part_features = features // groups
    place = jnp.stack([row, core, block])

    cut = part_features // 256 * 128
    shares = (0, cut)
    first, second = [
        [lax.dynamic_slice_in_dim(basis_store[0], group * part_features + start, size, 0)]
        for start, size in zip(shares, (cut, part_features - cut))
    ]
    flat_grads = after(gradients.reshape(slots, features), first[0], second[0])

    def share(index):
        return lax.dynamic_slice_in_dim(flat_grads, index * part_features, part_features, 1)

    away = [share((group + step) % groups) for step in range(1, groups)]
    others = [[shift(rows, "groups", step)] for step, rows in enumerate(away, 1)]

    flat_acts = activations.reshape(slots, activations.shape[2])
    act, *away_act = rotate(place, flat_acts, basis_act, blocks, cores)
    for step in range(1, dp):
        first.append(shift(first[-1], "dp", 1))
        second.append(shift(second[-1], "dp", 1))
        if step == 1:
            first[1], act, flat_grads, *away_act = lax.optimization_barrier(
                (first[1], act, flat_grads, *away_act)
            )
            away_act = [
                to_neighbour(part, i // cores, i % cores) for i, part in enumerate(away_act, 1)
            ]
            rows = [[share(group)]] + others
    act = after(act, first[2])
    for i, part in enumerate(away_act):
        act = act + (after(part, first[-1]) if i == 0 else part)
    pieces = [piece for pair in zip(first, second) for piece in pair]
    early = [early_products(part, pieces[:-4], shares) for part in rows]
    act_parts = gather_act(act.astype(BF16), (first[-1], early[0]))
    rest = [early_products(part, pieces[-4:-1], shares) for part in rows]
    act_rot_t = assemble(after(place, *early, *rest), act_parts, blocks, cores)
    last, act_rot_t, *done = lax.optimization_barrier((pieces[-1], act_rot_t, *early, *rest))
    early, rest = done[: len(rows)], done[len(rows) :]
    last, *sends = pack(owner_slot, place, rows, last, cut, early, rest, blocks, cores)
    came = [shift(send, "cores", step) for step, send in enumerate(sends, 1)]
    parts = join(owner_slot, place, last, early, rest, came, blocks, cores)

    parts = list(parts)
    for far in range(blocks):
        for back in range(groups):
            if far or back:
                pairs = [
                    (g * blocks + b, ((g - back) % groups) * blocks + (b + far) % blocks)
                    for g in range(groups)
                    for b in range(blocks)
                ]
                i = far * groups + back
                parts[i] = lax.ppermute(parts[i], ("groups", "block"), pairs)

    height = reader_blocks.shape[1] * BW // dp
    own, *others = squares(
        token_counts, reader_blocks, place, act_rot_t, parts, height, dp
    )
    for step in range(1, dp):
        own = own + shift(others[step - 1], "dp", step).astype(F32)
    return own / (seq_local * dp)


def solution(mesh):
    in_specs = (
        P(("groups", "dp"), None, ("block", "cores")),
        P(("groups", "dp"), None, ("block", "cores")),
        P(("groups", "dp")),
        P(("block", "cores"), None),
        P("dp", ("block", "cores"), None),
        P(),
        P(("block", "cores"), None),
    )
    out_specs = P(("groups", "dp"), ("block", "cores"))
    return jax.shard_map(
        on_device, mesh=mesh, in_specs=in_specs, out_specs=out_specs, check_vma=False
    )
```

```python
import functools

import jax
import jax.numpy as jnp
from jax import lax
from jax.experimental import pallas as pl
from jax.experimental.pallas import tpu as pltpu
from jax.sharding import PartitionSpec as P

BW = 512
LEN = 128
F32 = jnp.float32
BF16 = jnp.bfloat16
VMEM_LIMIT = 40 * 1024 * 1024
VMEM = pl.BlockSpec(memory_space=pltpu.VMEM)
SMEM = pl.BlockSpec(memory_space=pltpu.SMEM)


def after(value, *gates):
    return lax.optimization_barrier((value,) + gates)[0]


def shift(value, axis, step):
    size = lax.axis_size(axis)
    return lax.ppermute(value, axis, [(i, (i + step) % size) for i in range(size)])


def block_of(value, index):
    return lax.dynamic_index_in_dim(value, index, 0, keepdims=False)


def to_neighbour(value, far, step):
    cores, blocks = lax.axis_size("cores"), lax.axis_size("block")
    pairs = [
        (b * cores + c, (b + far) % blocks * cores + (c + step) % cores)
        for b in range(blocks)
        for c in range(cores)
    ]
    return lax.ppermute(value, ("block", "cores"), pairs)


def assemble_kernel(blocks, cores, place, *refs):
    parts, out = refs[:-1], refs[-1]
    height = parts[0].shape[0]
    for i, part in enumerate(parts):
        core = lax.rem(place[1] - i % cores + cores, cores)
        block = lax.rem(place[2] - i // cores + blocks, blocks)
        start = pl.multiple_of((core * blocks + block) * height, height)
        out[pl.ds(start, height)] = part[...]


def gather_act(act, gate):
    cores, blocks = lax.axis_size("cores"), lax.axis_size("block")
    sent = [after(act, *gate) if i == 1 else act for i in range(blocks * cores)]
    parts = [act] + [to_neighbour(sent[i], i // cores, i % cores) for i in range(1, len(sent))]
    return parts


def assemble(place, parts, blocks, cores):
    shape = (len(parts) * parts[0].shape[0], parts[0].shape[1])
    return pl.pallas_call(
        functools.partial(assemble_kernel, blocks, cores),
        out_shape=jax.ShapeDtypeStruct(shape, BF16),
        in_specs=[SMEM] + [VMEM] * len(parts),
        out_specs=VMEM,
        compiler_params=pltpu.CompilerParams(vmem_limit_bytes=VMEM_LIMIT),
    )(place, *parts)


def rotate_kernel(blocks, cores, place, acts, basis, *outs):
    height = outs[0].shape[0]
    for core_step in range(cores):
        core = lax.rem(place[1] + core_step, cores)
        span = blocks * height
        columns = pl.ds(pl.multiple_of(core * span, span), span)
        term = jnp.dot(acts[...], basis[:, columns], preferred_element_type=F32)
        for share in range(blocks):
            step = lax.rem(share - place[2] + blocks, blocks)
            part = term[:, share * height : (share + 1) * height].T
            for i in range(blocks):

                @pl.when(step == i)
                def _():
                    outs[i * cores + core_step][...] = part


def rotate(place, acts, basis, blocks, cores):
    shape = (basis.shape[1] // (blocks * cores), acts.shape[0])
    return pl.pallas_call(
        functools.partial(rotate_kernel, blocks, cores),
        out_shape=(jax.ShapeDtypeStruct(shape, F32),) * (blocks * cores),
        in_specs=[SMEM, VMEM, VMEM],
        out_specs=(VMEM,) * (blocks * cores),
        compiler_params=pltpu.CompilerParams(vmem_limit_bytes=VMEM_LIMIT),
    )(place, acts, basis)


def product(rows, piece, start):
    total, first = None, 0
    for part in rows:
        last = first + part.shape[1]
        low, high = max(first, start), min(last, start + piece.shape[0])
        if low < high:
            term = jnp.dot(
                part[:, low - first : high - first],
                piece[low - start : high - start],
                preferred_element_type=F32,
            )
            total = term if total is None else total + term
        first = last
    return total


def early_kernel(parts, shares, *refs):
    rows, pieces, out = refs[:parts], refs[parts:-1], refs[-1]
    for position in range(out.shape[0]):
        total = None
        for share, start in enumerate(shares):
            i = position * len(shares) + share
            if i < len(pieces):
                term = product(rows, pieces[i], start)
                total = term if total is None else total + term
        out[position] = total


def early_products(rows, pieces, shares):
    positions = -(-len(pieces) // len(shares))
    height, width = rows[0].shape[0], pieces[0].shape[1]
    flops = 2 * height * width * sum(piece.shape[0] for piece in pieces)
    return pl.pallas_call(
        functools.partial(early_kernel, len(rows), shares),
        out_shape=jax.ShapeDtypeStruct((positions, height, width), F32),
        in_specs=[VMEM] * (len(rows) + len(pieces)),
        out_specs=VMEM,
        compiler_params=pltpu.CompilerParams(vmem_limit_bytes=VMEM_LIMIT),
        cost_estimate=pl.CostEstimate(
            flops=flops, bytes_accessed=flops // width, transcendentals=0
        ),
    )(*rows, *pieces)


def total_of(position, early, rest, last, group):
    positions = early[0].shape[0]
    height = early[0].shape[1]
    at_last = last[pl.ds(group * height, height)]
    before = early[group][jnp.minimum(position, positions - 1)]
    late = jnp.where(position == positions, rest[group][0], at_last)
    return jnp.where(position < positions, before, late)


def pack_kernel(dp, cores, parts, start, owner, place, held, *refs):
    row, core = place[0], place[1]
    refs = list(refs)
    rows = [[refs.pop(0) for _ in range(cuts)] for cuts in parts]
    early = [refs.pop(0) for _ in parts]
    rest = [refs.pop(0) for _ in parts]
    last, sends = refs[0], refs[1:]
    height = early[0].shape[1]
    for g in range(len(parts)):
        last[g * height : (g + 1) * height] = rest[g][1] + product(rows[g], held, start)
    for step in range(1, cores):
        for block in range(sends[0].shape[0]):
            piece = block * cores + lax.rem(core + step, cores)
            position = lax.rem(row - owner[piece] + dp, dp)
            for g in range(len(parts)):
                sends[step - 1][block, g * height : (g + 1) * height] = total_of(
                    position, early, rest, last, g
                )


def pack(owner_slot, place, rows, held, start, early, rest, blocks, cores):
    positions, height, width = early[0].shape
    shape = (len(rows) * height, width)
    parts = tuple(len(part) for part in rows)
    return pl.pallas_call(
        functools.partial(pack_kernel, positions + 2, cores, parts, start),
        out_shape=(jax.ShapeDtypeStruct(shape, F32),)
        + (jax.ShapeDtypeStruct((blocks,) + shape, F32),) * (cores - 1),
        in_specs=[SMEM, SMEM] + [VMEM] * (1 + sum(parts) + 2 * len(rows)),
        out_specs=(VMEM,) * cores,
        compiler_params=pltpu.CompilerParams(vmem_limit_bytes=VMEM_LIMIT),
    )(owner_slot, place, held, *[cut for part in rows for cut in part], *early, *rest)


def join_kernel(dp, cores, groups, blocks, owner, place, last, *refs):
    row, core, me = place[0], place[1], place[2]
    early, rest, refs = refs[:groups], refs[groups : 2 * groups], refs[2 * groups :]
    came, outs = refs[: cores - 1], refs[cores - 1 :]
    height = early[0].shape[1]
    for far in range(blocks):
        block = lax.rem(me + far, blocks)
        position = lax.rem(row - owner[block * cores + core] + dp, dp)
        for g in range(groups):
            total = total_of(position, early, rest, last, g)
            for other in came:
                total = total + other[block, g * height : (g + 1) * height]
            outs[far * groups + g][...] = total


def join(owner_slot, place, last, early, rest, came, blocks, cores):
    positions, height, width = early[0].shape
    groups = len(early)
    return pl.pallas_call(
        functools.partial(join_kernel, positions + 2, cores, groups, blocks),
        out_shape=(jax.ShapeDtypeStruct((height, width), F32),) * (blocks * groups),
        in_specs=[SMEM, SMEM] + [VMEM] * (1 + 2 * groups + len(came)),
        out_specs=(VMEM,) * (blocks * groups),
        compiler_params=pltpu.CompilerParams(vmem_limit_bytes=VMEM_LIMIT),
    )(owner_slot, place, last, *early, *rest, *came)


def square_kernel(dp, terms, counts, wanted, place, act, *refs):
    parts, outs = refs[:terms], refs[terms:]
    row = place[0]
    total = parts[0][...]
    for part in parts[1:]:
        total = total + part[...]
    sequences = total.shape[0] // LEN
    rotated = []
    for s in range(sequences):
        position = lax.broadcasted_iota(jnp.int32, (LEN, total.shape[1]), 0)
        used = jnp.where(position < counts[s], total[s * LEN : (s + 1) * LEN], 0.0)
        rotated.append(used.astype(BF16))
    height = outs[0].shape[0]
    for step in range(dp):
        start = lax.rem(row + step, dp) * height
        first = wanted[0, start // BW] * BW + lax.rem(start, BW)
        rows = pl.ds(pl.multiple_of(first, height), height)
        square = None
        for s in range(sequences):
            product = jnp.dot(
                act[rows, s * LEN : (s + 1) * LEN], rotated[s], preferred_element_type=F32
            )
            square = product * product if square is None else square + product * product
        outs[step][...] = square.astype(outs[step].dtype)


def squares(counts, wanted, place, act, parts, height, dp):
    width = parts[0].shape[1]
    return pl.pallas_call(
        functools.partial(square_kernel, dp, len(parts)),
        out_shape=tuple(
            jax.ShapeDtypeStruct((height, width), F32 if step == 0 else BF16)
            for step in range(dp)
        ),
        in_specs=[SMEM, SMEM, SMEM, VMEM] + [VMEM] * len(parts),
        out_specs=(VMEM,) * dp,
        compiler_params=pltpu.CompilerParams(vmem_limit_bytes=VMEM_LIMIT),
    )(counts, wanted, place, act, *parts)


def on_device(
    activations, gradients, token_counts, basis_act, basis_store, owner_slot, reader_blocks
):
    seq_local = activations.shape[0]
    slots = seq_local * LEN
    groups, dp = lax.axis_size("groups"), lax.axis_size("dp")
    cores, blocks = lax.axis_size("cores"), lax.axis_size("block")
    group, row = lax.axis_index("groups"), lax.axis_index("dp")
    block, core = lax.axis_index("block"), lax.axis_index("cores")
    _, features, width = basis_store.shape
    part_features = features // groups
    place = jnp.stack([row, core, block])

    cut = part_features // 256 * 128
    shares = (0, cut)
    first, second = [
        [lax.dynamic_slice_in_dim(basis_store[0], group * part_features + start, size, 0)]
        for start, size in zip(shares, (cut, part_features - cut))
    ]
    flat_grads = after(gradients.reshape(slots, features), first[0], second[0])

    def share(index):
        return lax.dynamic_slice_in_dim(flat_grads, index * part_features, part_features, 1)

    away = [share((group + step) % groups) for step in range(1, groups)]
    others = [[shift(rows, "groups", step)] for step, rows in enumerate(away, 1)]

    flat_acts = activations.reshape(slots, activations.shape[2])
    act, *away_act = rotate(place, flat_acts, basis_act, blocks, cores)
    for step in range(1, dp):
        first.append(shift(first[-1], "dp", 1))
        second.append(shift(second[-1], "dp", 1))
        if step == 1:
            first[1], act, flat_grads, *away_act = lax.optimization_barrier(
                (first[1], act, flat_grads, *away_act)
            )
            away_act = [
                to_neighbour(part, i // cores, i % cores) for i, part in enumerate(away_act, 1)
            ]
            rows = [[share(group)]] + others
    act = after(act, first[2])
    for part in away_act:
        act = act + part
    pieces = [piece for pair in zip(first, second) for piece in pair]
    early = [early_products(part, pieces[:-4], shares) for part in rows]
    act_parts = gather_act(act.astype(BF16), (first[-1], early[0]))
    rest = [early_products(part, pieces[-4:-1], shares) for part in rows]
    act_rot_t = assemble(after(place, *early, *rest), act_parts, blocks, cores)
    last, act_rot_t, *done = lax.optimization_barrier((pieces[-1], act_rot_t, *early, *rest))
    early, rest = done[: len(rows)], done[len(rows) :]
    last, *sends = pack(owner_slot, place, rows, last, cut, early, rest, blocks, cores)
    came = [shift(send, "cores", step) for step, send in enumerate(sends, 1)]
    parts = join(owner_slot, place, last, early, rest, came, blocks, cores)

    parts = list(parts)
    for far in range(blocks):
        for back in range(groups):
            if far or back:
                pairs = [
                    (g * blocks + b, ((g - back) % groups) * blocks + (b + far) % blocks)
                    for g in range(groups)
                    for b in range(blocks)
                ]
                i = far * groups + back
                parts[i] = lax.ppermute(parts[i], ("groups", "block"), pairs)

    height = reader_blocks.shape[1] * BW // dp
    own, *others = squares(
        token_counts, reader_blocks, place, act_rot_t, parts, height, dp
    )
    for step in range(1, dp):
        own = own + shift(others[step - 1], "dp", step).astype(F32)
    return own / (seq_local * dp)


def solution(mesh):
    in_specs = (
        P(("groups", "dp"), None, ("block", "cores")),
        P(("groups", "dp"), None, ("block", "cores")),
        P(("groups", "dp")),
        P(("block", "cores"), None),
        P("dp", ("block", "cores"), None),
        P(),
        P(("block", "cores"), None),
    )
    out_specs = P(("groups", "dp"), ("block", "cores"))
    return jax.shard_map(
        on_device, mesh=mesh, in_specs=in_specs, out_specs=out_specs, check_vma=False
    )
```

```python
import functools

import jax
import jax.numpy as jnp
from jax import lax
from jax.experimental import pallas as pl
from jax.experimental.pallas import tpu as pltpu
from jax.sharding import PartitionSpec as P

BW = 512
LEN = 128
F32 = jnp.float32
BF16 = jnp.bfloat16
VMEM_LIMIT = 40 * 1024 * 1024
VMEM = pl.BlockSpec(memory_space=pltpu.VMEM)
SMEM = pl.BlockSpec(memory_space=pltpu.SMEM)


def after(value, *gates):
    return lax.optimization_barrier((value,) + gates)[0]


def shift(value, axis, step):
    size = lax.axis_size(axis)
    return lax.ppermute(value, axis, [(i, (i + step) % size) for i in range(size)])


def block_of(value, index):
    return lax.dynamic_index_in_dim(value, index, 0, keepdims=False)


def to_neighbour(value, far, step):
    cores, blocks = lax.axis_size("cores"), lax.axis_size("block")
    pairs = [
        (b * cores + c, (b + far) % blocks * cores + (c + step) % cores)
        for b in range(blocks)
        for c in range(cores)
    ]
    return lax.ppermute(value, ("block", "cores"), pairs)


def assemble_kernel(blocks, cores, place, *refs):
    parts, out = refs[:-1], refs[-1]
    height = parts[0].shape[0]
    for i, part in enumerate(parts):
        core = lax.rem(place[1] - i % cores + cores, cores)
        block = lax.rem(place[2] - i // cores + blocks, blocks)
        start = pl.multiple_of((core * blocks + block) * height, height)
        out[pl.ds(start, height)] = part[...]


def gather_act(act, gate):
    cores, blocks = lax.axis_size("cores"), lax.axis_size("block")
    sent = [after(act, *gate) if i == 1 else act for i in range(blocks * cores)]
    parts = [act] + [to_neighbour(sent[i], i // cores, i % cores) for i in range(1, len(sent))]
    return parts


def assemble(place, parts, blocks, cores):
    shape = (len(parts) * parts[0].shape[0], parts[0].shape[1])
    return pl.pallas_call(
        functools.partial(assemble_kernel, blocks, cores),
        out_shape=jax.ShapeDtypeStruct(shape, BF16),
        in_specs=[SMEM] + [VMEM] * len(parts),
        out_specs=VMEM,
        compiler_params=pltpu.CompilerParams(vmem_limit_bytes=VMEM_LIMIT),
    )(place, *parts)


def split_kernel(store, first, second, sems):
    size = first.shape[0] + second.shape[0]
    start = lax.axis_index("groups") * size
    copies = []
    for i, out in enumerate((first, second)):
        rows = pl.ds(pl.multiple_of(start + i * first.shape[0], 16), out.shape[0])
        copies.append(pltpu.make_async_copy(store.at[rows], out, sems.at[i]))
    for copy in copies:
        copy.start()
    for copy in copies:
        copy.wait()


def split(store, cut, size):
    return pl.pallas_call(
        split_kernel,
        out_shape=tuple(
            jax.ShapeDtypeStruct((rows, store.shape[1]), store.dtype) for rows in (cut, size - cut)
        ),
        in_specs=[pl.BlockSpec(memory_space=pltpu.HBM)],
        out_specs=(VMEM, VMEM),
        scratch_shapes=[pltpu.SemaphoreType.DMA((2,))],
        compiler_params=pltpu.CompilerParams(vmem_limit_bytes=VMEM_LIMIT),
    )(store)


def rotate_kernel(blocks, cores, place, acts, basis, *outs):
    height = outs[0].shape[0]
    for core_step in range(cores):
        core = lax.rem(place[1] + core_step, cores)
        span = blocks * height
        columns = pl.ds(pl.multiple_of(core * span, span), span)
        term = jnp.dot(acts[...], basis[:, columns], preferred_element_type=F32)
        for share in range(blocks):
            step = lax.rem(share - place[2] + blocks, blocks)
            part = term[:, share * height : (share + 1) * height].T
            for i in range(blocks):

                @pl.when(step == i)
                def _():
                    outs[i * cores + core_step][...] = part


def rotate(place, acts, basis, blocks, cores):
    shape = (basis.shape[1] // (blocks * cores), acts.shape[0])
    return pl.pallas_call(
        functools.partial(rotate_kernel, blocks, cores),
        out_shape=(jax.ShapeDtypeStruct(shape, F32),) * (blocks * cores),
        in_specs=[SMEM, VMEM, VMEM],
        out_specs=(VMEM,) * (blocks * cores),
        compiler_params=pltpu.CompilerParams(vmem_limit_bytes=VMEM_LIMIT),
    )(place, acts, basis)


def product(rows, piece, start):
    total, first = None, 0
    for part in rows:
        last = first + part.shape[1]
        low, high = max(first, start), min(last, start + piece.shape[0])
        if low < high:
            term = jnp.dot(
                part[:, low - first : high - first],
                piece[low - start : high - start],
                preferred_element_type=F32,
            )
            total = term if total is None else total + term
        first = last
    return total


def early_kernel(parts, shares, *refs):
    rows, pieces, out = refs[:parts], refs[parts:-1], refs[-1]
    for position in range(out.shape[0]):
        total = None
        for share, start in enumerate(shares):
            i = position * len(shares) + share
            if i < len(pieces):
                term = product(rows, pieces[i], start)
                total = term if total is None else total + term
        out[position] = total


def early_products(rows, pieces, shares):
    positions = -(-len(pieces) // len(shares))
    height, width = rows[0].shape[0], pieces[0].shape[1]
    flops = 2 * height * width * sum(piece.shape[0] for piece in pieces)
    return pl.pallas_call(
        functools.partial(early_kernel, len(rows), shares),
        out_shape=jax.ShapeDtypeStruct((positions, height, width), F32),
        in_specs=[VMEM] * (len(rows) + len(pieces)),
        out_specs=VMEM,
        compiler_params=pltpu.CompilerParams(vmem_limit_bytes=VMEM_LIMIT),
        cost_estimate=pl.CostEstimate(
            flops=flops, bytes_accessed=flops // width, transcendentals=0
        ),
    )(*rows, *pieces)


def total_of(position, early, rest, last, group):
    positions = early[0].shape[0]
    height = early[0].shape[1]
    at_last = last[pl.ds(group * height, height)]
    before = early[group][jnp.minimum(position, positions - 1)]
    late = jnp.where(position == positions, rest[group][0], at_last)
    return jnp.where(position < positions, before, late)


def pack_kernel(dp, cores, parts, start, owner, place, held, *refs):
    row, core = place[0], place[1]
    refs = list(refs)
    rows = [[refs.pop(0) for _ in range(cuts)] for cuts in parts]
    early = [refs.pop(0) for _ in parts]
    rest = [refs.pop(0) for _ in parts]
    last, sends = refs[0], refs[1:]
    height = early[0].shape[1]
    for g in range(len(parts)):
        last[g * height : (g + 1) * height] = rest[g][1] + product(rows[g], held, start)
    for step in range(1, cores):
        for block in range(sends[0].shape[0]):
            piece = block * cores + lax.rem(core + step, cores)
            position = lax.rem(row - owner[piece] + dp, dp)
            for g in range(len(parts)):
                sends[step - 1][block, g * height : (g + 1) * height] = total_of(
                    position, early, rest, last, g
                )


def pack(owner_slot, place, rows, held, start, early, rest, blocks, cores):
    positions, height, width = early[0].shape
    shape = (len(rows) * height, width)
    parts = tuple(len(part) for part in rows)
    return pl.pallas_call(
        functools.partial(pack_kernel, positions + 2, cores, parts, start),
        out_shape=(jax.ShapeDtypeStruct(shape, F32),)
        + (jax.ShapeDtypeStruct((blocks,) + shape, F32),) * (cores - 1),
        in_specs=[SMEM, SMEM] + [VMEM] * (1 + sum(parts) + 2 * len(rows)),
        out_specs=(VMEM,) * cores,
        compiler_params=pltpu.CompilerParams(vmem_limit_bytes=VMEM_LIMIT),
    )(owner_slot, place, held, *[cut for part in rows for cut in part], *early, *rest)


def join_kernel(dp, cores, groups, blocks, owner, place, last, *refs):
    row, core, me = place[0], place[1], place[2]
    early, rest, refs = refs[:groups], refs[groups : 2 * groups], refs[2 * groups :]
    came, outs = refs[: cores - 1], refs[cores - 1 :]
    height = early[0].shape[1]
    for far in range(blocks):
        block = lax.rem(me + far, blocks)
        position = lax.rem(row - owner[block * cores + core] + dp, dp)
        for g in range(groups):
            total = total_of(position, early, rest, last, g)
            for other in came:
                total = total + other[block, g * height : (g + 1) * height]
            outs[far * groups + g][...] = total


def join(owner_slot, place, last, early, rest, came, blocks, cores):
    positions, height, width = early[0].shape
    groups = len(early)
    return pl.pallas_call(
        functools.partial(join_kernel, positions + 2, cores, groups, blocks),
        out_shape=(jax.ShapeDtypeStruct((height, width), F32),) * (blocks * groups),
        in_specs=[SMEM, SMEM] + [VMEM] * (1 + 2 * groups + len(came)),
        out_specs=(VMEM,) * (blocks * groups),
        compiler_params=pltpu.CompilerParams(vmem_limit_bytes=VMEM_LIMIT),
    )(owner_slot, place, last, *early, *rest, *came)


def square_kernel(dp, terms, counts, wanted, place, act, *refs):
    parts, outs = refs[:terms], refs[terms:]
    row = place[0]
    total = parts[0][...]
    for part in parts[1:]:
        total = total + part[...]
    sequences = total.shape[0] // LEN
    rotated = []
    for s in range(sequences):
        position = lax.broadcasted_iota(jnp.int32, (LEN, total.shape[1]), 0)
        used = jnp.where(position < counts[s], total[s * LEN : (s + 1) * LEN], 0.0)
        rotated.append(used.astype(BF16))
    height = outs[0].shape[0]
    for step in range(dp):
        start = lax.rem(row + step, dp) * height
        first = wanted[0, start // BW] * BW + lax.rem(start, BW)
        rows = pl.ds(pl.multiple_of(first, height), height)
        square = None
        for s in range(sequences):
            product = jnp.dot(
                act[rows, s * LEN : (s + 1) * LEN], rotated[s], preferred_element_type=F32
            )
            square = product * product if square is None else square + product * product
        outs[step][...] = square.astype(outs[step].dtype)


def squares(counts, wanted, place, act, parts, height, dp):
    width = parts[0].shape[1]
    return pl.pallas_call(
        functools.partial(square_kernel, dp, len(parts)),
        out_shape=tuple(
            jax.ShapeDtypeStruct((height, width), F32 if step == 0 else BF16)
            for step in range(dp)
        ),
        in_specs=[SMEM, SMEM, SMEM, VMEM] + [VMEM] * len(parts),
        out_specs=(VMEM,) * dp,
        compiler_params=pltpu.CompilerParams(vmem_limit_bytes=VMEM_LIMIT),
    )(counts, wanted, place, act, *parts)


def on_device(
    activations, gradients, token_counts, basis_act, basis_store, owner_slot, reader_blocks
):
    seq_local = activations.shape[0]
    slots = seq_local * LEN
    groups, dp = lax.axis_size("groups"), lax.axis_size("dp")
    cores, blocks = lax.axis_size("cores"), lax.axis_size("block")
    group, row = lax.axis_index("groups"), lax.axis_index("dp")
    block, core = lax.axis_index("block"), lax.axis_index("cores")
    _, features, width = basis_store.shape
    part_features = features // groups
    place = jnp.stack([row, core, block])

    cut = part_features // 256 * 128
    shares = (0, cut)
    first, second = [[part] for part in split(basis_store[0], cut, part_features)]
    flat_grads = after(gradients.reshape(slots, features), first[0], second[0])

    def share(index):
        return lax.dynamic_slice_in_dim(flat_grads, index * part_features, part_features, 1)

    away = [share((group + step) % groups) for step in range(1, groups)]
    others = [[shift(rows, "groups", step)] for step, rows in enumerate(away, 1)]

    flat_acts = activations.reshape(slots, activations.shape[2])
    act, *away_act = rotate(place, flat_acts, basis_act, blocks, cores)
    for step in range(1, dp):
        first.append(shift(first[-1], "dp", 1))
        second.append(shift(second[-1], "dp", 1))
        if step == 1:
            first[1], act, flat_grads, *away_act = lax.optimization_barrier(
                (first[1], act, flat_grads, *away_act)
            )
            away_act = [
                to_neighbour(part, i // cores, i % cores) for i, part in enumerate(away_act, 1)
            ]
            rows = [[share(group)]] + others
    act = after(act, first[2])
    for part in away_act:
        act = act + part
    pieces = [piece for pair in zip(first, second) for piece in pair]
    early = [early_products(part, pieces[:-4], shares) for part in rows]
    act_parts = gather_act(act.astype(BF16), (first[-1], early[0]))
    rest = [early_products(part, pieces[-4:-1], shares) for part in rows]
    act_rot_t = assemble(after(place, *early, *rest), act_parts, blocks, cores)
    last, act_rot_t, *done = lax.optimization_barrier((pieces[-1], act_rot_t, *early, *rest))
    early, rest = done[: len(rows)], done[len(rows) :]
    last, *sends = pack(owner_slot, place, rows, last, cut, early, rest, blocks, cores)
    came = [shift(send, "cores", step) for step, send in enumerate(sends, 1)]
    parts = join(owner_slot, place, last, early, rest, came, blocks, cores)

    parts = list(parts)
    for far in range(blocks):
        for back in range(groups):
            if far or back:
                pairs = [
                    (g * blocks + b, ((g - back) % groups) * blocks + (b + far) % blocks)
                    for g in range(groups)
                    for b in range(blocks)
                ]
                i = far * groups + back
                parts[i] = lax.ppermute(parts[i], ("groups", "block"), pairs)

    height = reader_blocks.shape[1] * BW // dp
    own, *others = squares(
        token_counts, reader_blocks, place, act_rot_t, parts, height, dp
    )
    for step in range(1, dp):
        own = own + shift(others[step - 1], "dp", step).astype(F32)
    return own / (seq_local * dp)


def solution(mesh):
    in_specs = (
        P(("groups", "dp"), None, ("block", "cores")),
        P(("groups", "dp"), None, ("block", "cores")),
        P(("groups", "dp")),
        P(("block", "cores"), None),
        P("dp", ("block", "cores"), None),
        P(),
        P(("block", "cores"), None),
    )
    out_specs = P(("groups", "dp"), ("block", "cores"))
    return jax.shard_map(
        on_device, mesh=mesh, in_specs=in_specs, out_specs=out_specs, check_vma=False
    )
```

```python
import functools

import jax
import jax.numpy as jnp
from jax import lax
from jax.experimental import pallas as pl
from jax.experimental.pallas import tpu as pltpu
from jax.sharding import PartitionSpec as P

BW = 512
LEN = 128
F32 = jnp.float32
BF16 = jnp.bfloat16
VMEM_LIMIT = 40 * 1024 * 1024
VMEM = pl.BlockSpec(memory_space=pltpu.VMEM)
SMEM = pl.BlockSpec(memory_space=pltpu.SMEM)


def after(value, *gates):
    return lax.optimization_barrier((value,) + gates)[0]


def shift(value, axis, step):
    size = lax.axis_size(axis)
    return lax.ppermute(value, axis, [(i, (i + step) % size) for i in range(size)])


def block_of(value, index):
    return lax.dynamic_index_in_dim(value, index, 0, keepdims=False)


def to_neighbour(value, far, step):
    cores, blocks = lax.axis_size("cores"), lax.axis_size("block")
    pairs = [
        (b * cores + c, (b + far) % blocks * cores + (c + step) % cores)
        for b in range(blocks)
        for c in range(cores)
    ]
    return lax.ppermute(value, ("block", "cores"), pairs)


def assemble_kernel(blocks, cores, place, *refs):
    parts, out = refs[:-1], refs[-1]
    height = parts[0].shape[0]
    for i, part in enumerate(parts):
        core = lax.rem(place[1] - i % cores + cores, cores)
        block = lax.rem(place[2] - i // cores + blocks, blocks)
        start = pl.multiple_of((core * blocks + block) * height, height)
        out[pl.ds(start, height)] = part[...]


def gather_act(act, gate):
    cores, blocks = lax.axis_size("cores"), lax.axis_size("block")
    sent = [after(act, *gate) if i == 1 else act for i in range(blocks * cores)]
    parts = [act] + [to_neighbour(sent[i], i // cores, i % cores) for i in range(1, len(sent))]
    return parts


def assemble(place, parts, blocks, cores):
    shape = (len(parts) * parts[0].shape[0], parts[0].shape[1])
    return pl.pallas_call(
        functools.partial(assemble_kernel, blocks, cores),
        out_shape=jax.ShapeDtypeStruct(shape, BF16),
        in_specs=[SMEM] + [VMEM] * len(parts),
        out_specs=VMEM,
        compiler_params=pltpu.CompilerParams(vmem_limit_bytes=VMEM_LIMIT),
    )(place, *parts)


def split_kernel(store, first, second, sems):
    size = first.shape[0] + second.shape[0]
    start = lax.axis_index("groups") * size
    copies = []
    for i, out in enumerate((first, second)):
        rows = pl.ds(pl.multiple_of(start + i * first.shape[0], 16), out.shape[0])
        copies.append(pltpu.make_async_copy(store.at[rows], out, sems.at[i]))
    for copy in copies:
        copy.start()
    for copy in copies:
        copy.wait()


def split(store, cut, size):
    return pl.pallas_call(
        split_kernel,
        out_shape=tuple(
            jax.ShapeDtypeStruct((rows, store.shape[1]), store.dtype) for rows in (cut, size - cut)
        ),
        in_specs=[pl.BlockSpec(memory_space=pltpu.HBM)],
        out_specs=(VMEM, VMEM),
        scratch_shapes=[pltpu.SemaphoreType.DMA((2,))],
    )(store)


def rotate_kernel(blocks, cores, place, acts, basis, *outs):
    height = outs[0].shape[0]
    for core_step in range(cores):
        core = lax.rem(place[1] + core_step, cores)
        span = blocks * height
        columns = pl.ds(pl.multiple_of(core * span, span), span)
        term = jnp.dot(acts[...], basis[:, columns], preferred_element_type=F32)
        for share in range(blocks):
            step = lax.rem(share - place[2] + blocks, blocks)
            part = term[:, share * height : (share + 1) * height].T
            for i in range(blocks):

                @pl.when(step == i)
                def _():
                    outs[i * cores + core_step][...] = part


def rotate(place, acts, basis, blocks, cores):
    shape = (basis.shape[1] // (blocks * cores), acts.shape[0])
    return pl.pallas_call(
        functools.partial(rotate_kernel, blocks, cores),
        out_shape=(jax.ShapeDtypeStruct(shape, F32),) * (blocks * cores),
        in_specs=[SMEM, VMEM, VMEM],
        out_specs=(VMEM,) * (blocks * cores),
        compiler_params=pltpu.CompilerParams(vmem_limit_bytes=VMEM_LIMIT),
    )(place, acts, basis)


def product(rows, piece, start):
    total, first = None, 0
    for part in rows:
        last = first + part.shape[1]
        low, high = max(first, start), min(last, start + piece.shape[0])
        if low < high:
            term = jnp.dot(
                part[:, low - first : high - first],
                piece[low - start : high - start],
                preferred_element_type=F32,
            )
            total = term if total is None else total + term
        first = last
    return total


def early_kernel(parts, shares, *refs):
    rows, pieces, out = refs[:parts], refs[parts:-1], refs[-1]
    for position in range(out.shape[0]):
        total = None
        for share, start in enumerate(shares):
            i = position * len(shares) + share
            if i < len(pieces):
                term = product(rows, pieces[i], start)
                total = term if total is None else total + term
        out[position] = total


def early_products(rows, pieces, shares):
    positions = -(-len(pieces) // len(shares))
    height, width = rows[0].shape[0], pieces[0].shape[1]
    flops = 2 * height * width * sum(piece.shape[0] for piece in pieces)
    return pl.pallas_call(
        functools.partial(early_kernel, len(rows), shares),
        out_shape=jax.ShapeDtypeStruct((positions, height, width), F32),
        in_specs=[VMEM] * (len(rows) + len(pieces)),
        out_specs=VMEM,
        compiler_params=pltpu.CompilerParams(vmem_limit_bytes=VMEM_LIMIT),
        cost_estimate=pl.CostEstimate(
            flops=flops, bytes_accessed=flops // width, transcendentals=0
        ),
    )(*rows, *pieces)


def total_of(position, early, rest, last, group):
    positions = early[0].shape[0]
    height = early[0].shape[1]
    at_last = last[pl.ds(group * height, height)]
    before = early[group][jnp.minimum(position, positions - 1)]
    late = jnp.where(position == positions, rest[group][0], at_last)
    return jnp.where(position < positions, before, late)


def pack_kernel(dp, cores, parts, start, owner, place, held, *refs):
    row, core = place[0], place[1]
    refs = list(refs)
    rows = [[refs.pop(0) for _ in range(cuts)] for cuts in parts]
    early = [refs.pop(0) for _ in parts]
    rest = [refs.pop(0) for _ in parts]
    last, sends = refs[0], refs[1:]
    height = early[0].shape[1]
    for g in range(len(parts)):
        last[g * height : (g + 1) * height] = rest[g][1] + product(rows[g], held, start)
    for step in range(1, cores):
        for block in range(sends[0].shape[0]):
            piece = block * cores + lax.rem(core + step, cores)
            position = lax.rem(row - owner[piece] + dp, dp)
            for g in range(len(parts)):
                sends[step - 1][block, g * height : (g + 1) * height] = total_of(
                    position, early, rest, last, g
                )


def pack(owner_slot, place, rows, held, start, early, rest, blocks, cores):
    positions, height, width = early[0].shape
    shape = (len(rows) * height, width)
    parts = tuple(len(part) for part in rows)
    return pl.pallas_call(
        functools.partial(pack_kernel, positions + 2, cores, parts, start),
        out_shape=(jax.ShapeDtypeStruct(shape, F32),)
        + (jax.ShapeDtypeStruct((blocks,) + shape, F32),) * (cores - 1),
        in_specs=[SMEM, SMEM] + [VMEM] * (1 + sum(parts) + 2 * len(rows)),
        out_specs=(VMEM,) * cores,
        compiler_params=pltpu.CompilerParams(vmem_limit_bytes=VMEM_LIMIT),
    )(owner_slot, place, held, *[cut for part in rows for cut in part], *early, *rest)


def join_kernel(dp, cores, groups, blocks, owner, place, last, *refs):
    row, core, me = place[0], place[1], place[2]
    early, rest, refs = refs[:groups], refs[groups : 2 * groups], refs[2 * groups :]
    came, outs = refs[: cores - 1], refs[cores - 1 :]
    height = early[0].shape[1]
    for far in range(blocks):
        block = lax.rem(me + far, blocks)
        position = lax.rem(row - owner[block * cores + core] + dp, dp)
        for g in range(groups):
            total = total_of(position, early, rest, last, g)
            for other in came:
                total = total + other[block, g * height : (g + 1) * height]
            outs[far * groups + g][...] = total


def join(owner_slot, place, last, early, rest, came, blocks, cores):
    positions, height, width = early[0].shape
    groups = len(early)
    return pl.pallas_call(
        functools.partial(join_kernel, positions + 2, cores, groups, blocks),
        out_shape=(jax.ShapeDtypeStruct((height, width), F32),) * (blocks * groups),
        in_specs=[SMEM, SMEM] + [VMEM] * (1 + 2 * groups + len(came)),
        out_specs=(VMEM,) * (blocks * groups),
        compiler_params=pltpu.CompilerParams(vmem_limit_bytes=VMEM_LIMIT),
    )(owner_slot, place, last, *early, *rest, *came)


def square_kernel(dp, terms, counts, wanted, place, act, *refs):
    parts, outs = refs[:terms], refs[terms:]
    row = place[0]
    total = parts[0][...]
    for part in parts[1:]:
        total = total + part[...]
    sequences = total.shape[0] // LEN
    rotated = []
    for s in range(sequences):
        position = lax.broadcasted_iota(jnp.int32, (LEN, total.shape[1]), 0)
        used = jnp.where(position < counts[s], total[s * LEN : (s + 1) * LEN], 0.0)
        rotated.append(used.astype(BF16))
    height = outs[0].shape[0]
    for step in range(dp):
        start = lax.rem(row + step, dp) * height
        first = wanted[0, start // BW] * BW + lax.rem(start, BW)
        rows = pl.ds(pl.multiple_of(first, height), height)
        square = None
        for s in range(sequences):
            product = jnp.dot(
                act[rows, s * LEN : (s + 1) * LEN], rotated[s], preferred_element_type=F32
            )
            square = product * product if square is None else square + product * product
        outs[step][...] = square.astype(outs[step].dtype)


def squares(counts, wanted, place, act, parts, height, dp):
    width = parts[0].shape[1]
    return pl.pallas_call(
        functools.partial(square_kernel, dp, len(parts)),
        out_shape=tuple(
            jax.ShapeDtypeStruct((height, width), F32 if step == 0 else BF16)
            for step in range(dp)
        ),
        in_specs=[SMEM, SMEM, SMEM, VMEM] + [VMEM] * len(parts),
        out_specs=(VMEM,) * dp,
        compiler_params=pltpu.CompilerParams(vmem_limit_bytes=VMEM_LIMIT),
    )(counts, wanted, place, act, *parts)


def on_device(
    activations, gradients, token_counts, basis_act, basis_store, owner_slot, reader_blocks
):
    seq_local = activations.shape[0]
    slots = seq_local * LEN
    groups, dp = lax.axis_size("groups"), lax.axis_size("dp")
    cores, blocks = lax.axis_size("cores"), lax.axis_size("block")
    group, row = lax.axis_index("groups"), lax.axis_index("dp")
    block, core = lax.axis_index("block"), lax.axis_index("cores")
    _, features, width = basis_store.shape
    part_features = features // groups
    place = jnp.stack([row, core, block])

    cut = part_features // 256 * 128
    shares = (0, cut)
    first, second = [[part] for part in split(basis_store[0], cut, part_features)]
    flat_grads = after(gradients.reshape(slots, features), first[0], second[0])

    def share(index):
        return lax.dynamic_slice_in_dim(flat_grads, index * part_features, part_features, 1)

    away = [share((group + step) % groups) for step in range(1, groups)]
    others = [[shift(rows, "groups", step)] for step, rows in enumerate(away, 1)]

    flat_acts = activations.reshape(slots, activations.shape[2])
    act, *away_act = rotate(place, flat_acts, basis_act, blocks, cores)
    for step in range(1, dp):
        first.append(shift(first[-1], "dp", 1))
        second.append(shift(second[-1], "dp", 1))
        if step == 1:
            first[1], act, flat_grads, *away_act = lax.optimization_barrier(
                (first[1], act, flat_grads, *away_act)
            )
            away_act = [
                to_neighbour(part, i // cores, i % cores) for i, part in enumerate(away_act, 1)
            ]
            rows = [[share(group)]] + others
    act = after(act, first[2])
    for part in away_act:
        act = act + part
    pieces = [piece for pair in zip(first, second) for piece in pair]
    early = [early_products(part, pieces[:-4], shares) for part in rows]
    act_parts = gather_act(act.astype(BF16), (first[-1], early[0]))
    rest = [early_products(part, pieces[-4:-1], shares) for part in rows]
    act_rot_t = assemble(after(place, *early, *rest), act_parts, blocks, cores)
    last, act_rot_t, *done = lax.optimization_barrier((pieces[-1], act_rot_t, *early, *rest))
    early, rest = done[: len(rows)], done[len(rows) :]
    last, *sends = pack(owner_slot, place, rows, last, cut, early, rest, blocks, cores)
    came = [shift(send, "cores", step) for step, send in enumerate(sends, 1)]
    parts = join(owner_slot, place, last, early, rest, came, blocks, cores)

    parts = list(parts)
    for far in range(blocks):
        for back in range(groups):
            if far or back:
                pairs = [
                    (g * blocks + b, ((g - back) % groups) * blocks + (b + far) % blocks)
                    for g in range(groups)
                    for b in range(blocks)
                ]
                i = far * groups + back
                parts[i] = lax.ppermute(parts[i], ("groups", "block"), pairs)

    height = reader_blocks.shape[1] * BW // dp
    own, *others = squares(
        token_counts, reader_blocks, place, act_rot_t, parts, height, dp
    )
    for step in range(1, dp):
        own = own + shift(others[step - 1], "dp", step).astype(F32)
    return own / (seq_local * dp)


def solution(mesh):
    in_specs = (
        P(("groups", "dp"), None, ("block", "cores")),
        P(("groups", "dp"), None, ("block", "cores")),
        P(("groups", "dp")),
        P(("block", "cores"), None),
        P("dp", ("block", "cores"), None),
        P(),
        P(("block", "cores"), None),
    )
    out_specs = P(("groups", "dp"), ("block", "cores"))
    return jax.shard_map(
        on_device, mesh=mesh, in_specs=in_specs, out_specs=out_specs, check_vma=False
    )
```

```python
import functools

import jax
import jax.numpy as jnp
from jax import lax
from jax.experimental import pallas as pl
from jax.experimental.pallas import tpu as pltpu
from jax.sharding import PartitionSpec as P

BW = 512
LEN = 128
F32 = jnp.float32
BF16 = jnp.bfloat16
VMEM_LIMIT = 40 * 1024 * 1024
VMEM = pl.BlockSpec(memory_space=pltpu.VMEM)
SMEM = pl.BlockSpec(memory_space=pltpu.SMEM)


def after(value, *gates):
    return lax.optimization_barrier((value,) + gates)[0]


def shift(value, axis, step):
    size = lax.axis_size(axis)
    return lax.ppermute(value, axis, [(i, (i + step) % size) for i in range(size)])


def block_of(value, index):
    return lax.dynamic_index_in_dim(value, index, 0, keepdims=False)


def to_neighbour(value, far, step):
    cores, blocks = lax.axis_size("cores"), lax.axis_size("block")
    pairs = [
        (b * cores + c, (b + far) % blocks * cores + (c + step) % cores)
        for b in range(blocks)
        for c in range(cores)
    ]
    return lax.ppermute(value, ("block", "cores"), pairs)


def assemble_kernel(blocks, cores, place, *refs):
    parts, out = refs[:-1], refs[-1]
    height = parts[0].shape[0]
    for i, part in enumerate(parts):
        core = lax.rem(place[1] - i % cores + cores, cores)
        block = lax.rem(place[2] - i // cores + blocks, blocks)
        start = pl.multiple_of((core * blocks + block) * height, height)
        out[pl.ds(start, height)] = part[...]


def gather_act(act, gate):
    cores, blocks = lax.axis_size("cores"), lax.axis_size("block")
    sent = [after(act, *gate) if i == 1 else act for i in range(blocks * cores)]
    parts = [act] + [to_neighbour(sent[i], i // cores, i % cores) for i in range(1, len(sent))]
    return parts


def assemble(place, parts, blocks, cores):
    shape = (len(parts) * parts[0].shape[0], parts[0].shape[1])
    return pl.pallas_call(
        functools.partial(assemble_kernel, blocks, cores),
        out_shape=jax.ShapeDtypeStruct(shape, BF16),
        in_specs=[SMEM] + [VMEM] * len(parts),
        out_specs=VMEM,
        compiler_params=pltpu.CompilerParams(vmem_limit_bytes=VMEM_LIMIT),
    )(place, *parts)


def rotate_kernel(blocks, cores, place, acts, basis, *outs):
    height = outs[0].shape[0]
    for core_step in range(cores):
        core = lax.rem(place[1] + core_step, cores)
        span = blocks * height
        columns = pl.ds(pl.multiple_of(core * span, span), span)
        term = jnp.dot(acts[...], basis[:, columns], preferred_element_type=F32)
        for share in range(blocks):
            step = lax.rem(share - place[2] + blocks, blocks)
            part = term[:, share * height : (share + 1) * height].T
            for i in range(blocks):

                @pl.when(step == i)
                def _():
                    outs[i * cores + core_step][...] = part


def rotate(place, acts, basis, blocks, cores):
    shape = (basis.shape[1] // (blocks * cores), acts.shape[0])
    return pl.pallas_call(
        functools.partial(rotate_kernel, blocks, cores),
        out_shape=(jax.ShapeDtypeStruct(shape, F32),) * (blocks * cores),
        in_specs=[SMEM, VMEM, VMEM],
        out_specs=(VMEM,) * (blocks * cores),
        compiler_params=pltpu.CompilerParams(vmem_limit_bytes=VMEM_LIMIT),
    )(place, acts, basis)


def product(rows, piece, start):
    total, first = None, 0
    for part in rows:
        last = first + part.shape[1]
        low, high = max(first, start), min(last, start + piece.shape[0])
        if low < high:
            term = jnp.dot(
                part[:, low - first : high - first],
                piece[low - start : high - start],
                preferred_element_type=F32,
            )
            total = term if total is None else total + term
        first = last
    return total


def early_kernel(parts, shares, *refs):
    rows, pieces, out = refs[:parts], refs[parts:-1], refs[-1]
    for position in range(out.shape[0]):
        total = None
        for share, start in enumerate(shares):
            i = position * len(shares) + share
            if i < len(pieces):
                term = product(rows, pieces[i], start)
                total = term if total is None else total + term
        out[position] = total


def early_products(rows, pieces, shares):
    positions = -(-len(pieces) // len(shares))
    height, width = rows[0].shape[0], pieces[0].shape[1]
    flops = 2 * height * width * sum(piece.shape[0] for piece in pieces)
    return pl.pallas_call(
        functools.partial(early_kernel, len(rows), shares),
        out_shape=jax.ShapeDtypeStruct((positions, height, width), F32),
        in_specs=[VMEM] * (len(rows) + len(pieces)),
        out_specs=VMEM,
        compiler_params=pltpu.CompilerParams(vmem_limit_bytes=VMEM_LIMIT),
        cost_estimate=pl.CostEstimate(
            flops=flops, bytes_accessed=flops // width, transcendentals=0
        ),
    )(*rows, *pieces)


def total_of(position, early, rest, last, group):
    positions = early[0].shape[0]
    height = early[0].shape[1]
    at_last = last[pl.ds(group * height, height)]
    before = early[group][jnp.minimum(position, positions - 1)]
    late = jnp.where(position == positions, rest[group][0], at_last)
    return jnp.where(position < positions, before, late)


def pack_kernel(dp, cores, parts, start, owner, place, held, *refs):
    row, core = place[0], place[1]
    refs = list(refs)
    rows = [[refs.pop(0) for _ in range(cuts)] for cuts in parts]
    early = [refs.pop(0) for _ in parts]
    rest = [refs.pop(0) for _ in parts]
    last, sends = refs[0], refs[1:]
    height = early[0].shape[1]
    for g in range(len(parts)):
        last[g * height : (g + 1) * height] = rest[g][1] + product(rows[g], held, start)
    for step in range(1, cores):
        for block in range(sends[0].shape[0]):
            piece = block * cores + lax.rem(core + step, cores)
            position = lax.rem(row - owner[piece] + dp, dp)
            for g in range(len(parts)):
                sends[step - 1][block, g * height : (g + 1) * height] = total_of(
                    position, early, rest, last, g
                )


def pack(owner_slot, place, rows, held, start, early, rest, blocks, cores):
    positions, height, width = early[0].shape
    shape = (len(rows) * height, width)
    parts = tuple(len(part) for part in rows)
    return pl.pallas_call(
        functools.partial(pack_kernel, positions + 2, cores, parts, start),
        out_shape=(jax.ShapeDtypeStruct(shape, F32),)
        + (jax.ShapeDtypeStruct((blocks,) + shape, F32),) * (cores - 1),
        in_specs=[SMEM, SMEM] + [VMEM] * (1 + sum(parts) + 2 * len(rows)),
        out_specs=(VMEM,) * cores,
        compiler_params=pltpu.CompilerParams(vmem_limit_bytes=VMEM_LIMIT),
    )(owner_slot, place, held, *[cut for part in rows for cut in part], *early, *rest)


def join_kernel(dp, cores, groups, blocks, owner, place, last, *refs):
    row, core, me = place[0], place[1], place[2]
    early, rest, refs = refs[:groups], refs[groups : 2 * groups], refs[2 * groups :]
    came, outs = refs[: cores - 1], refs[cores - 1 :]
    height = early[0].shape[1]
    for far in range(blocks):
        block = lax.rem(me + far, blocks)
        position = lax.rem(row - owner[block * cores + core] + dp, dp)
        for g in range(groups):
            total = total_of(position, early, rest, last, g)
            for other in came:
                total = total + other[block, g * height : (g + 1) * height]
            outs[far * groups + g][...] = total


def join(owner_slot, place, last, early, rest, came, blocks, cores):
    positions, height, width = early[0].shape
    groups = len(early)
    return pl.pallas_call(
        functools.partial(join_kernel, positions + 2, cores, groups, blocks),
        out_shape=(jax.ShapeDtypeStruct((height, width), F32),) * (blocks * groups),
        in_specs=[SMEM, SMEM] + [VMEM] * (1 + 2 * groups + len(came)),
        out_specs=(VMEM,) * (blocks * groups),
        compiler_params=pltpu.CompilerParams(vmem_limit_bytes=VMEM_LIMIT),
    )(owner_slot, place, last, *early, *rest, *came)


def square_kernel(dp, terms, counts, wanted, place, act, *refs):
    parts, outs = refs[:terms], refs[terms:]
    row = place[0]
    total = parts[0][...]
    for part in parts[1:]:
        total = total + part[...]
    sequences = total.shape[0] // LEN
    rotated = []
    for s in range(sequences):
        position = lax.broadcasted_iota(jnp.int32, (LEN, total.shape[1]), 0)
        used = jnp.where(position < counts[s], total[s * LEN : (s + 1) * LEN], 0.0)
        rotated.append(used.astype(BF16))
    height = outs[0].shape[0]
    for step in range(dp):
        start = lax.rem(row + step, dp) * height
        first = wanted[0, start // BW] * BW + lax.rem(start, BW)
        rows = pl.ds(pl.multiple_of(first, height), height)
        square = None
        for s in range(sequences):
            product = jnp.dot(
                act[rows, s * LEN : (s + 1) * LEN], rotated[s], preferred_element_type=F32
            )
            square = product * product if square is None else square + product * product
        outs[step][...] = square.astype(outs[step].dtype)


def squares(counts, wanted, place, act, parts, height, dp):
    width = parts[0].shape[1]
    return pl.pallas_call(
        functools.partial(square_kernel, dp, len(parts)),
        out_shape=tuple(
            jax.ShapeDtypeStruct((height, width), F32 if step == 0 else BF16)
            for step in range(dp)
        ),
        in_specs=[SMEM, SMEM, SMEM, VMEM] + [VMEM] * len(parts),
        out_specs=(VMEM,) * dp,
        compiler_params=pltpu.CompilerParams(vmem_limit_bytes=VMEM_LIMIT),
    )(counts, wanted, place, act, *parts)


def on_device(
    activations, gradients, token_counts, basis_act, basis_store, owner_slot, reader_blocks
):
    seq_local = activations.shape[0]
    slots = seq_local * LEN
    groups, dp = lax.axis_size("groups"), lax.axis_size("dp")
    cores, blocks = lax.axis_size("cores"), lax.axis_size("block")
    group, row = lax.axis_index("groups"), lax.axis_index("dp")
    block, core = lax.axis_index("block"), lax.axis_index("cores")
    _, features, width = basis_store.shape
    part_features = features // groups
    place = jnp.stack([row, core, block])

    cut = part_features // 256 * 128
    shares = (0, cut)
    first, second = [
        [lax.dynamic_slice_in_dim(basis_store[0], group * part_features + start, size, 0)]
        for start, size in zip(shares, (cut, part_features - cut))
    ]
    flat_grads = after(gradients.reshape(slots, features), first[0], second[0])

    def share(index):
        return lax.dynamic_slice_in_dim(flat_grads, index * part_features, part_features, 1)

    away = [share((group + step) % groups) for step in range(1, groups)]
    others = [[shift(rows, "groups", step)] for step, rows in enumerate(away, 1)]

    flat_acts = activations.reshape(slots, activations.shape[2])
    act, *away_act = rotate(place, flat_acts, basis_act, blocks, cores)
    for step in range(1, dp):
        first.append(shift(first[-1], "dp", 1))
        second.append(shift(second[-1], "dp", 1))
        if step == 1:
            first[1], act, flat_grads, *away_act = lax.optimization_barrier(
                (first[1], act, flat_grads, *away_act)
            )
            away_act = [
                to_neighbour(part, i // cores, i % cores) for i, part in enumerate(away_act, 1)
            ]
            rows = [[share(group)]] + others
    act = after(act, first[2])
    for part in away_act:
        act = act + part
    pieces = [piece for pair in zip(first, second) for piece in pair]
    early = [early_products(part, pieces[:-4], shares) for part in rows]
    act_parts = gather_act(act.astype(BF16), (first[-1], early[0]))
    rest = [early_products(part, pieces[-4:-1], shares) for part in rows]
    act_rot_t = assemble(after(place, *early, *rest), act_parts, blocks, cores)
    ends = [part[0][:, cut:] for part in rows]
    last, act_rot_t, *done = lax.optimization_barrier(
        (pieces[-1], act_rot_t, *early, *rest, *ends)
    )
    early, rest, ends = (done[i * len(rows) : (i + 1) * len(rows)] for i in range(3))
    ends = [[part] for part in ends]
    last, *sends = pack(owner_slot, place, ends, last, 0, early, rest, blocks, cores)
    came = [shift(send, "cores", step) for step, send in enumerate(sends, 1)]
    parts = join(owner_slot, place, last, early, rest, came, blocks, cores)

    parts = list(parts)
    for far in range(blocks):
        for back in range(groups):
            if far or back:
                pairs = [
                    (g * blocks + b, ((g - back) % groups) * blocks + (b + far) % blocks)
                    for g in range(groups)
                    for b in range(blocks)
                ]
                i = far * groups + back
                parts[i] = lax.ppermute(parts[i], ("groups", "block"), pairs)

    height = reader_blocks.shape[1] * BW // dp
    own, *others = squares(
        token_counts, reader_blocks, place, act_rot_t, parts, height, dp
    )
    for step in range(1, dp):
        own = own + shift(others[step - 1], "dp", step).astype(F32)
    return own / (seq_local * dp)


def solution(mesh):
    in_specs = (
        P(("groups", "dp"), None, ("block", "cores")),
        P(("groups", "dp"), None, ("block", "cores")),
        P(("groups", "dp")),
        P(("block", "cores"), None),
        P("dp", ("block", "cores"), None),
        P(),
        P(("block", "cores"), None),
    )
    out_specs = P(("groups", "dp"), ("block", "cores"))
    return jax.shard_map(
        on_device, mesh=mesh, in_specs=in_specs, out_specs=out_specs, check_vma=False
    )
```

```python
import functools

import jax
import jax.numpy as jnp
from jax import lax
from jax.experimental import pallas as pl
from jax.experimental.pallas import tpu as pltpu
from jax.sharding import PartitionSpec as P

BW = 512
LEN = 128
F32 = jnp.float32
BF16 = jnp.bfloat16
VMEM_LIMIT = 40 * 1024 * 1024
VMEM = pl.BlockSpec(memory_space=pltpu.VMEM)
SMEM = pl.BlockSpec(memory_space=pltpu.SMEM)


def after(value, *gates):
    return lax.optimization_barrier((value,) + gates)[0]


def shift(value, axis, step):
    size = lax.axis_size(axis)
    return lax.ppermute(value, axis, [(i, (i + step) % size) for i in range(size)])


def block_of(value, index):
    return lax.dynamic_index_in_dim(value, index, 0, keepdims=False)


def to_neighbour(value, far, step):
    cores, blocks = lax.axis_size("cores"), lax.axis_size("block")
    pairs = [
        (b * cores + c, (b + far) % blocks * cores + (c + step) % cores)
        for b in range(blocks)
        for c in range(cores)
    ]
    return lax.ppermute(value, ("block", "cores"), pairs)


def assemble_kernel(blocks, cores, place, *refs):
    parts, out = refs[:-1], refs[-1]
    height = parts[0].shape[0]
    for i, part in enumerate(parts):
        core = lax.rem(place[1] - i % cores + cores, cores)
        block = lax.rem(place[2] - i // cores + blocks, blocks)
        start = pl.multiple_of((core * blocks + block) * height, height)
        out[pl.ds(start, height)] = part[...]


def gather_act(act, gate):
    cores, blocks = lax.axis_size("cores"), lax.axis_size("block")
    sent = [after(act, *gate) if i == 1 else act for i in range(blocks * cores)]
    parts = [act] + [to_neighbour(sent[i], i // cores, i % cores) for i in range(1, len(sent))]
    return parts


def assemble(place, parts, blocks, cores):
    shape = (len(parts) * parts[0].shape[0], parts[0].shape[1])
    return pl.pallas_call(
        functools.partial(assemble_kernel, blocks, cores),
        out_shape=jax.ShapeDtypeStruct(shape, BF16),
        in_specs=[SMEM] + [VMEM] * len(parts),
        out_specs=VMEM,
        compiler_params=pltpu.CompilerParams(vmem_limit_bytes=VMEM_LIMIT),
    )(place, *parts)


def rotate_kernel(blocks, cores, place, acts, basis, *outs):
    height = outs[0].shape[0]
    for core_step in range(cores):
        core = lax.rem(place[1] + core_step, cores)
        span = blocks * height
        columns = pl.ds(pl.multiple_of(core * span, span), span)
        term = jnp.dot(acts[...], basis[:, columns], preferred_element_type=F32)
        for share in range(blocks):
            step = lax.rem(share - place[2] + blocks, blocks)
            part = term[:, share * height : (share + 1) * height].T
            for i in range(blocks):

                @pl.when(step == i)
                def _():
                    outs[i * cores + core_step][...] = part


def rotate(place, acts, basis, blocks, cores):
    shape = (basis.shape[1] // (blocks * cores), acts.shape[0])
    return pl.pallas_call(
        functools.partial(rotate_kernel, blocks, cores),
        out_shape=(jax.ShapeDtypeStruct(shape, F32),) * (blocks * cores),
        in_specs=[SMEM, VMEM, VMEM],
        out_specs=(VMEM,) * (blocks * cores),
        compiler_params=pltpu.CompilerParams(vmem_limit_bytes=VMEM_LIMIT),
    )(place, acts, basis)


def product(rows, piece, start):
    total, first = None, 0
    for part in rows:
        last = first + part.shape[1]
        low, high = max(first, start), min(last, start + piece.shape[0])
        if low < high:
            term = jnp.dot(
                part[:, low - first : high - first],
                piece[low - start : high - start],
                preferred_element_type=F32,
            )
            total = term if total is None else total + term
        first = last
    return total


def early_kernel(parts, shares, *refs):
    rows, pieces, out = refs[:parts], refs[parts:-1], refs[-1]
    for position in range(out.shape[0]):
        total = None
        for share, start in enumerate(shares):
            i = position * len(shares) + share
            if i < len(pieces):
                term = product(rows, pieces[i], start)
                total = term if total is None else total + term
        out[position] = total


def early_products(rows, pieces, shares):
    positions = -(-len(pieces) // len(shares))
    height, width = rows[0].shape[0], pieces[0].shape[1]
    flops = 2 * height * width * sum(piece.shape[0] for piece in pieces)
    return pl.pallas_call(
        functools.partial(early_kernel, len(rows), shares),
        out_shape=jax.ShapeDtypeStruct((positions, height, width), F32),
        in_specs=[VMEM] * (len(rows) + len(pieces)),
        out_specs=VMEM,
        compiler_params=pltpu.CompilerParams(vmem_limit_bytes=VMEM_LIMIT),
        cost_estimate=pl.CostEstimate(
            flops=flops, bytes_accessed=flops // width, transcendentals=0
        ),
    )(*rows, *pieces)


def total_of(position, early, rest, last, group):
    positions = early[0].shape[0]
    height = early[0].shape[1]
    at_last = last[pl.ds(group * height, height)]
    before = early[group][jnp.minimum(position, positions - 1)]
    late = jnp.where(position == positions, rest[group][0], at_last)
    return jnp.where(position < positions, before, late)


def pack_kernel(dp, cores, parts, start, owner, place, held, *refs):
    row, core = place[0], place[1]
    refs = list(refs)
    rows = [[refs.pop(0) for _ in range(cuts)] for cuts in parts]
    early = [refs.pop(0) for _ in parts]
    rest = [refs.pop(0) for _ in parts]
    last, sends = refs[0], refs[1:]
    height = early[0].shape[1]
    for g in range(len(parts)):
        last[g * height : (g + 1) * height] = rest[g][1] + product(rows[g], held, start if g == 0 else 0)
    for step in range(1, cores):
        for block in range(sends[0].shape[0]):
            piece = block * cores + lax.rem(core + step, cores)
            position = lax.rem(row - owner[piece] + dp, dp)
            for g in range(len(parts)):
                sends[step - 1][block, g * height : (g + 1) * height] = total_of(
                    position, early, rest, last, g
                )


def pack(owner_slot, place, rows, held, start, early, rest, blocks, cores):
    positions, height, width = early[0].shape
    shape = (len(rows) * height, width)
    parts = tuple(len(part) for part in rows)
    return pl.pallas_call(
        functools.partial(pack_kernel, positions + 2, cores, parts, start),
        out_shape=(jax.ShapeDtypeStruct(shape, F32),)
        + (jax.ShapeDtypeStruct((blocks,) + shape, F32),) * (cores - 1),
        in_specs=[SMEM, SMEM] + [VMEM] * (1 + sum(parts) + 2 * len(rows)),
        out_specs=(VMEM,) * cores,
        compiler_params=pltpu.CompilerParams(vmem_limit_bytes=VMEM_LIMIT),
    )(owner_slot, place, held, *[cut for part in rows for cut in part], *early, *rest)


def join_kernel(dp, cores, groups, blocks, owner, place, last, *refs):
    row, core, me = place[0], place[1], place[2]
    early, rest, refs = refs[:groups], refs[groups : 2 * groups], refs[2 * groups :]
    came, outs = refs[: cores - 1], refs[cores - 1 :]
    height = early[0].shape[1]
    for far in range(blocks):
        block = lax.rem(me + far, blocks)
        position = lax.rem(row - owner[block * cores + core] + dp, dp)
        for g in range(groups):
            total = total_of(position, early, rest, last, g)
            for other in came:
                total = total + other[block, g * height : (g + 1) * height]
            outs[far * groups + g][...] = total


def join(owner_slot, place, last, early, rest, came, blocks, cores):
    positions, height, width = early[0].shape
    groups = len(early)
    return pl.pallas_call(
        functools.partial(join_kernel, positions + 2, cores, groups, blocks),
        out_shape=(jax.ShapeDtypeStruct((height, width), F32),) * (blocks * groups),
        in_specs=[SMEM, SMEM] + [VMEM] * (1 + 2 * groups + len(came)),
        out_specs=(VMEM,) * (blocks * groups),
        compiler_params=pltpu.CompilerParams(vmem_limit_bytes=VMEM_LIMIT),
    )(owner_slot, place, last, *early, *rest, *came)


def square_kernel(dp, terms, counts, wanted, place, act, *refs):
    parts, outs = refs[:terms], refs[terms:]
    row = place[0]
    total = parts[0][...]
    for part in parts[1:]:
        total = total + part[...]
    sequences = total.shape[0] // LEN
    rotated = []
    for s in range(sequences):
        position = lax.broadcasted_iota(jnp.int32, (LEN, total.shape[1]), 0)
        used = jnp.where(position < counts[s], total[s * LEN : (s + 1) * LEN], 0.0)
        rotated.append(used.astype(BF16))
    height = outs[0].shape[0]
    for step in range(dp):
        start = lax.rem(row + step, dp) * height
        first = wanted[0, start // BW] * BW + lax.rem(start, BW)
        rows = pl.ds(pl.multiple_of(first, height), height)
        square = None
        for s in range(sequences):
            product = jnp.dot(
                act[rows, s * LEN : (s + 1) * LEN], rotated[s], preferred_element_type=F32
            )
            square = product * product if square is None else square + product * product
        outs[step][...] = square.astype(outs[step].dtype)


def squares(counts, wanted, place, act, parts, height, dp):
    width = parts[0].shape[1]
    return pl.pallas_call(
        functools.partial(square_kernel, dp, len(parts)),
        out_shape=tuple(
            jax.ShapeDtypeStruct((height, width), F32 if step == 0 else BF16)
            for step in range(dp)
        ),
        in_specs=[SMEM, SMEM, SMEM, VMEM] + [VMEM] * len(parts),
        out_specs=(VMEM,) * dp,
        compiler_params=pltpu.CompilerParams(vmem_limit_bytes=VMEM_LIMIT),
    )(counts, wanted, place, act, *parts)


def on_device(
    activations, gradients, token_counts, basis_act, basis_store, owner_slot, reader_blocks
):
    seq_local = activations.shape[0]
    slots = seq_local * LEN
    groups, dp = lax.axis_size("groups"), lax.axis_size("dp")
    cores, blocks = lax.axis_size("cores"), lax.axis_size("block")
    group, row = lax.axis_index("groups"), lax.axis_index("dp")
    block, core = lax.axis_index("block"), lax.axis_index("cores")
    _, features, width = basis_store.shape
    part_features = features // groups
    place = jnp.stack([row, core, block])

    cut = part_features // 256 * 128
    shares = (0, cut)
    first, second = [
        [lax.dynamic_slice_in_dim(basis_store[0], group * part_features + start, size, 0)]
        for start, size in zip(shares, (cut, part_features - cut))
    ]
    flat_grads = after(gradients.reshape(slots, features), first[0], second[0])

    def share(index):
        return lax.dynamic_slice_in_dim(flat_grads, index * part_features, part_features, 1)

    away = [share((group + step) % groups) for step in range(1, groups)]
    others = [[shift(rows, "groups", step)] for step, rows in enumerate(away, 1)]

    flat_acts = activations.reshape(slots, activations.shape[2])
    act, *away_act = rotate(place, flat_acts, basis_act, blocks, cores)
    for step in range(1, dp):
        first.append(shift(first[-1], "dp", 1))
        second.append(shift(second[-1], "dp", 1))
        if step == 1:
            first[1], act, flat_grads, *away_act = lax.optimization_barrier(
                (first[1], act, flat_grads, *away_act)
            )
            away_act = [
                to_neighbour(part, i // cores, i % cores) for i, part in enumerate(away_act, 1)
            ]
            rows = [[share(group)]] + others
    act = after(act, first[2])
    for part in away_act:
        act = act + part
    pieces = [piece for pair in zip(first, second) for piece in pair]
    early = [early_products(part, pieces[:-4], shares) for part in rows]
    act_parts = gather_act(act.astype(BF16), (first[-1], early[0]))
    rest = [early_products(part, pieces[-4:-1], shares) for part in rows]
    act_rot_t = assemble(after(place, *early, *rest), act_parts, blocks, cores)
    ends = [rows[0][0]] + [part[0][:, cut:] for part in rows[1:]]
    last, act_rot_t, *done = lax.optimization_barrier(
        (pieces[-1], act_rot_t, *early, *rest, *ends)
    )
    early, rest, ends = (done[i * len(rows) : (i + 1) * len(rows)] for i in range(3))
    ends = [[part] for part in ends]
    last, *sends = pack(owner_slot, place, ends, last, cut, early, rest, blocks, cores)
    came = [shift(send, "cores", step) for step, send in enumerate(sends, 1)]
    parts = join(owner_slot, place, last, early, rest, came, blocks, cores)

    parts = list(parts)
    for far in range(blocks):
        for back in range(groups):
            if far or back:
                pairs = [
                    (g * blocks + b, ((g - back) % groups) * blocks + (b + far) % blocks)
                    for g in range(groups)
                    for b in range(blocks)
                ]
                i = far * groups + back
                parts[i] = lax.ppermute(parts[i], ("groups", "block"), pairs)

    height = reader_blocks.shape[1] * BW // dp
    own, *others = squares(
        token_counts, reader_blocks, place, act_rot_t, parts, height, dp
    )
    for step in range(1, dp):
        own = own + shift(others[step - 1], "dp", step).astype(F32)
    return own / (seq_local * dp)


def solution(mesh):
    in_specs = (
        P(("groups", "dp"), None, ("block", "cores")),
        P(("groups", "dp"), None, ("block", "cores")),
        P(("groups", "dp")),
        P(("block", "cores"), None),
        P("dp", ("block", "cores"), None),
        P(),
        P(("block", "cores"), None),
    )
    out_specs = P(("groups", "dp"), ("block", "cores"))
    return jax.shard_map(
        on_device, mesh=mesh, in_specs=in_specs, out_specs=out_specs, check_vma=False
    )
```
